512 devices in a mesh: dp: 8 (over y), tile: 64 (over z, x, core).
Axes of the slice: x: 4, y: 8, z: 8, core: 2. Of those that a mesh axis runs over, the one named last changes fastest.
Arguments:
- hidden: bfloat16 [512, 729, 1152], P(('dp', 'tile')), may hold values from -6 to 6
- norm_gain: float32 [1152], replicated, may hold values from 0.1 to 1.9
- norm_bias: float32 [1152], replicated, may hold values from -3 to 3
- slot_tile: int32 [512], P(('dp', 'tile')), may hold values from -1 to 55, as said below
- block_owner: int32 [8, 4, 27, 9], P('dp'), may hold values from 0 to 1023, as said below
- proj_weight: bfloat16 [3456, 2048], P('tile', 'dp'), may hold values from -0.109375 to 0.109375
- proj_grad: bfloat16 [64, 384, 2048], P('tile', None, 'dp'), may hold values from -0.59765625 to 0.59765625
Outputs:
- projected: bfloat16 [64, 384, 2048], P('tile', None, 'dp')
- weight_grad: float32 [3456, 2048], P('tile', 'dp')
- hidden_grad: bfloat16 [512, 729, 1152], P(('dp', 'tile'))
- gain_grad: float32 [1152], replicated
- bias_grad: float32 [1152], replicated
The draws below stay inside these ranges and needn't reach their ends.
Inputs may be any that keep to these rules, and one draw needn't show every extreme that they name: `slot_tile`: in each group's 64 * 1 entries (groups in dp order, devices in tile order, then slots) every tile number 0 to 55 stands exactly once and -1 elsewhere. `block_owner`: A value o names owner o // 16 along tile within the group and its slot o % 16. The values of one group are distinct; an owner holds at most 16 blocks and at most 4 blocks of one image, and both bounds are reached in every group.
All inputs are finite; a program needn't handle non-finite values.
Results may differ from the reference program's by a relative error of at most 0.018.
Values may be sent and summed in bfloat16 or wider, within the bound.
No kernel may reach another device: no remote copies, remote signals or barrier semaphores. Data moves between devices by JAX's collectives and lax.ppermute only.
A program may use at most 64 MiB of HBM per device.

```python
import jax
import jax.numpy as jnp
from jax import lax

WIDTH = 1152
PROJ = 2048
GRID = 27
BLOCK = 3
TILES_IMG = 14
IMAGES = 4
FEAT = 3456
TOKENS_TILE = 729
OWN = 16
TILES = 512
ROWS = 384
N_DP = 8
N_TILE = 64


def draw_slot_tile(key, part):
    key = jax.random.fold_in(key, 11)
    per_group = TILES // N_DP
    tile_total = IMAGES * TILES_IMG

    def one_group(group_key):
        slot_order = jax.random.permutation(group_key, per_group).astype(jnp.int32)
        inverse_order = jnp.argsort(slot_order).astype(jnp.int32)
        return jnp.where(inverse_order < tile_total, inverse_order, -1).astype(jnp.int32)
    split_keys = jax.random.split(key, N_DP)
    return jax.vmap(one_group)(split_keys).reshape(TILES).astype(jnp.int32)


def draw_block_owner(key, part):
    key = jax.random.fold_in(key, 23)
    block_count = GRID * (GRID // BLOCK)
    per_owner = block_count // N_TILE
    extra_count = block_count % N_TILE
    own_slots = IMAGES * per_owner + (IMAGES * extra_count + N_TILE - 1) // N_TILE
    owner_ids = jnp.arange(N_TILE, dtype=jnp.int32)
    copy_ids = jnp.arange(per_owner + 1, dtype=jnp.int32)
    cand_owner = jnp.broadcast_to(owner_ids[:, None], (N_TILE, per_owner + 1)).reshape(-1)
    cand_copy = jnp.broadcast_to(copy_ids[None, :], (N_TILE, per_owner + 1)).reshape(-1)
    cand_total = N_TILE * (per_owner + 1)

    def entries(extra_mask, first_slot, entry_key):
        usable = (cand_copy < per_owner) | extra_mask[cand_owner]
        sort_score = jnp.where(usable, 0, 1) * cand_total + jnp.arange(cand_total, dtype=jnp.int32)
        picked = jnp.argsort(sort_score)[:block_count]
        shuffled = picked[jax.random.permutation(entry_key, block_count)]
        owner_pick = cand_owner[shuffled]
        return (owner_pick * own_slots + first_slot[owner_pick] + cand_copy[shuffled]).astype(jnp.int32)

    def one_group(group_key):
        split_keys = jax.random.split(group_key, IMAGES + 1)
        ranking = jax.random.permutation(split_keys[0], N_TILE).astype(jnp.int32)
        start_slot = jnp.zeros((N_TILE,), jnp.int32)
        image_rows = []
        for image_idx in range(IMAGES):
            extra_mask = (ranking - image_idx * extra_count) % N_TILE < extra_count
            image_rows.append(entries(extra_mask, start_slot, split_keys[image_idx + 1]))
            start_slot = start_slot + per_owner + extra_mask.astype(jnp.int32)
        return jnp.stack(image_rows).reshape(IMAGES, GRID, GRID // BLOCK)
    group_keys = jax.random.split(key, N_DP)
    return jax.vmap(one_group)(group_keys).astype(jnp.int32)


def level_of(own_key, dims, shards, smallest, top_value):
    level, own = 1.0, jax.random.fold_in(own_key, 6)
    for position, shards_of in shards:
        draws = jnp.exp(jax.random.uniform(jax.random.fold_in(own, position), (shards_of,), jnp.float32, smallest / len(shards), top_value / len(shards)))
        level = level * jnp.repeat(draws, dims[position] // shards_of).reshape([-1 if axis == position else 1 for axis in range(len(dims))])
    return level


def noise(rng, dims, deviation, reach, shards=(), kind=jnp.bfloat16):
    factor_of = level_of(rng, dims, shards, -0.22, 0.18) if shards else 1.0
    drawn = jax.random.normal(rng, dims, jnp.float32) * deviation * factor_of
    return jnp.minimum(jnp.maximum(drawn, -reach), reach).astype(kind)


def setup_inputs(seed: int = 0) -> dict:
    splits = jax.random.split(jax.random.key(seed), 8)
    hidden = noise(splits[0], (TILES, TOKENS_TILE, WIDTH), 1.0, 6.0, ((0, 512),))
    norm_gain = jnp.clip(1.0 + 0.18 * jax.random.normal(splits[1], (WIDTH,), jnp.float32), 0.1, 1.9)
    norm_bias = noise(splits[2], (WIDTH,), 0.5, 3.0, (), jnp.float32)
    slot_tile = draw_slot_tile(jax.random.fold_in(splits[7], 71), 0)
    block_owner = draw_block_owner(jax.random.fold_in(splits[7], 71), 0)
    proj_weight = noise(splits[5], (FEAT, PROJ), FEAT ** -0.5, 0.109375, ((0, 64), (1, 8)))
    proj_grad = noise(splits[6], (N_TILE, ROWS, PROJ), 0.1, 0.59765625, ((0, 64), (2, 8)))
    return dict(hidden=hidden, norm_gain=norm_gain, norm_bias=norm_bias, slot_tile=slot_tile, block_owner=block_owner, proj_weight=proj_weight, proj_grad=proj_grad)


epsilon = 1e-06
highest_precision = lax.Precision.HIGHEST

def tile_shape(local_idx):
    tile_scale = jnp.where(local_idx == 0, 1, jnp.where(local_idx < 5, 2, 3)).astype(jnp.int32)
    within = jnp.where(local_idx < 5, local_idx - 1, local_idx - 5)
    tile_row = jnp.where(local_idx == 0, 0, within // tile_scale).astype(jnp.int32)
    tile_col = jnp.where(local_idx == 0, 0, within % tile_scale).astype(jnp.int32)
    return (tile_scale, tile_row, tile_col)

def pool_matrix(tile_scale, offset, is_live):
    cell_ids = jnp.arange(GRID, dtype=jnp.int32)
    target = (GRID * offset + cell_ids) // tile_scale
    matches = (target[None, :] == cell_ids[:, None]) & is_live
    weight_value = 1.0 / tile_scale.astype(jnp.float32)
    return jnp.where(matches, weight_value, 0.0).astype(jnp.float32)

def norm_forward(tokens_in, norm_gain, norm_bias):
    values = tokens_in.astype(jnp.float32)
    centered = values - lax.optimization_barrier(jnp.mean(values, axis=-1, keepdims=True))
    inverse_scale = lax.rsqrt(lax.optimization_barrier(jnp.mean(centered * centered, axis=-1, keepdims=True)) + epsilon)
    unit_rows = centered * inverse_scale
    return (unit_rows * norm_gain + norm_bias, unit_rows, inverse_scale)

def norm_backward(upstream, unit_rows, inverse_scale, norm_gain):
    scaled = upstream * norm_gain
    width_mean = lax.optimization_barrier(jnp.mean(scaled, axis=-1, keepdims=True))
    cross_mean = lax.optimization_barrier(jnp.mean(scaled * unit_rows, axis=-1, keepdims=True))
    return inverse_scale * (scaled - width_mean - unit_rows * cross_mean)

def reference(hidden, norm_gain, norm_bias, slot_tile, block_owner, proj_weight, proj_grad):
    per_group = TILES // N_DP
    bands = GRID // BLOCK
    zero_idx = jnp.zeros((), jnp.int32)

    def geometry(slot_idx):
        tile_id = slot_tile[slot_idx]
        is_live = tile_id >= 0
        safe_id = jnp.maximum(tile_id, 0)
        tile_scale, tile_row, tile_col = tile_shape(safe_id % TILES_IMG)
        row_pool = pool_matrix(tile_scale, tile_row, is_live)
        col_pool = pool_matrix(tile_scale, tile_col, is_live)
        corner = ((slot_idx // per_group).astype(jnp.int32), (safe_id // TILES_IMG).astype(jnp.int32), zero_idx, zero_idx, (tile_scale - 1).astype(jnp.int32), zero_idx)
        return (corner, row_pool, col_pool)

    def add_tile(features, slot_idx):
        corner, row_pool, col_pool = geometry(slot_idx)
        normed, unit_rows, inverse_scale = norm_forward(hidden[slot_idx], norm_gain, norm_bias)
        grid_values = normed.reshape(GRID, GRID, WIDTH)
        row_pooled = jnp.einsum('ra,abw->rbw', row_pool, grid_values, precision=highest_precision)
        pooled = jnp.einsum('cb,rbw->rcw', col_pool, row_pooled, precision=highest_precision)
        contribution = lax.optimization_barrier(pooled.astype(jnp.bfloat16)).astype(jnp.float32)
        current = lax.dynamic_slice(features, corner, (1, 1, GRID, GRID, 1, WIDTH))
        updated = current + contribution.reshape(1, 1, GRID, GRID, 1, WIDTH)
        return (lax.dynamic_update_slice(features, updated, corner), None)
    slot_ids = jnp.arange(TILES, dtype=jnp.int32)
    features = jnp.zeros((N_DP, IMAGES, GRID, GRID, 3, WIDTH), jnp.float32)
    features, unused = lax.scan(add_tile, features, slot_ids)
    features = features.astype(jnp.bfloat16)
    blocks = features.reshape(N_DP, IMAGES * GRID * bands, BLOCK, FEAT)
    owner_ids = block_owner.reshape(N_DP, IMAGES * GRID * bands)
    group_ids = jnp.arange(N_DP, dtype=jnp.int32)[:, None]
    owned = jnp.zeros((N_DP, N_TILE * OWN, BLOCK, FEAT), jnp.bfloat16).at[group_ids, owner_ids].set(blocks)
    owner_rows = owned.reshape(N_DP, N_TILE, OWN * BLOCK, FEAT).transpose(1, 0, 2, 3).reshape(N_TILE * ROWS, FEAT)
    upstream = proj_grad.reshape(N_TILE * ROWS, PROJ)
    projected = jnp.dot(owner_rows, proj_weight, preferred_element_type=jnp.float32)
    projected = projected.astype(jnp.bfloat16).reshape(N_TILE, ROWS, PROJ)
    weight_grad = jnp.dot(owner_rows.T, upstream, preferred_element_type=jnp.float32)
    group_cols = PROJ // N_DP
    row_sum = jnp.zeros((N_TILE * ROWS, FEAT), jnp.float32)
    for column_group in range(N_DP):
        upstream_part = upstream[:, column_group * group_cols:(column_group + 1) * group_cols]
        weight_part = proj_weight[:, column_group * group_cols:(column_group + 1) * group_cols]
        partial_sum = jnp.dot(upstream_part, weight_part.T, preferred_element_type=jnp.float32)
        row_sum = row_sum + lax.optimization_barrier(partial_sum.astype(jnp.bfloat16)).astype(jnp.float32)
    row_grad = row_sum.astype(jnp.bfloat16)
    owned_grad = row_grad.reshape(N_TILE, N_DP, OWN * BLOCK, FEAT).transpose(1, 0, 2, 3)
    owned_grad = owned_grad.reshape(N_DP, N_TILE * OWN, BLOCK, FEAT)
    feature_grad = owned_grad[group_ids, owner_ids].reshape(N_DP, IMAGES, GRID, GRID, 3, WIDTH)

    def back_tile(totals, slot_idx):
        corner, row_pool, col_pool = geometry(slot_idx)
        normed, unit_rows, inverse_scale = norm_forward(hidden[slot_idx], norm_gain, norm_bias)
        frame_grad = lax.dynamic_slice(feature_grad, corner, (1, 1, GRID, GRID, 1, WIDTH))
        frame_grad = frame_grad.reshape(GRID, GRID, WIDTH).astype(jnp.float32)
        col_back = jnp.einsum('cb,rcw->rbw', col_pool, frame_grad, precision=highest_precision)
        token_grad = jnp.einsum('ra,rbw->abw', row_pool, col_back, precision=highest_precision)
        token_grad = token_grad.reshape(GRID * GRID, WIDTH)
        hidden_grad = norm_backward(token_grad, unit_rows, inverse_scale, norm_gain).astype(jnp.bfloat16)
        totals = (totals[0] + lax.optimization_barrier(jnp.sum(token_grad * unit_rows, axis=0)), totals[1] + lax.optimization_barrier(jnp.sum(token_grad, axis=0)))
        return (totals, hidden_grad)
    initial = (jnp.zeros((WIDTH,), jnp.float32), jnp.zeros((WIDTH,), jnp.float32))
    (gain_grad, bias_grad), hidden_grad = lax.scan(back_tile, initial, slot_ids)
    return (projected, weight_grad, hidden_grad, gain_grad, bias_grad)
```

```python
import jax
import jax.numpy as jnp
from jax import lax
from jax.experimental import pallas as pl
from jax.experimental.pallas import tpu as pltpu
from jax.sharding import Mesh, PartitionSpec as P

GRID = 27
BLOCK = 3
TILES_IMG = 14
IMAGES = 4
WIDTH = 1152
TOKENS = GRID * GRID
BLOCKS = GRID * (GRID // BLOCK)
BLOCKS_PAD = 256
NZ, NX, NC = 8, 4, 2
PEERS = NZ * NX * NC
CAP = 4
SEND = PEERS * CAP
OWN = 16
OWN_ROWS = OWN * BLOCK
SHARD = 54
SHARD_PAD = 56
CHUNK = 192
STEPS = 4
ROWS = 32
EPS = 1e-6
VMEM = 48 * 1024 * 1024

f32 = jnp.float32
bf16 = jnp.bfloat16
i32 = jnp.int32


def iota(shape, dim):
    return lax.broadcasted_iota(i32, shape, dim)


def tile_geometry(tile):
    safe = jnp.maximum(tile, 0)
    image = lax.div(safe, TILES_IMG)
    local = safe - image * TILES_IMG
    scale = jnp.where(local == 0, 1, jnp.where(local < 5, 2, 3))
    within = jnp.where(local == 0, 0, jnp.where(local < 5, local - 1, local - 5))
    row = jnp.where(scale == 1, 0, jnp.where(scale == 2, within >> 1, lax.div(within, 3)))
    return image, scale, row, within - row * scale


def weight_of(scale):
    return jnp.where(scale == 1, 1.0, jnp.where(scale == 2, 1.0 / 4.0, 1.0 / 9.0)).astype(f32)


def third(x):
    return (x * 171) >> 9


def token_cells(token, scale, row, col):
    u = (token * 2428) >> 16
    v = token - u * GRID
    down, right = GRID * row + u, GRID * col + v
    r = jnp.where(scale == 1, down, jnp.where(scale == 2, down >> 1, third(down)))
    c = jnp.where(scale == 1, right, jnp.where(scale == 2, right >> 1, third(right)))
    band = third(c)
    return r * (GRID // BLOCK) + band, c - band * BLOCK


def pick_image(image, parts):
    out = jnp.where(image == 0, parts[0], 0)
    for i in range(1, IMAGES):
        out = out + jnp.where(image == i, parts[i], 0)
    return out


def same_owner(image, peer_row_ref, peer_col_ref):
    row = pick_image(image, [peer_row_ref[i : i + 1, :] for i in range(IMAGES)])
    col = pick_image(image, [peer_col_ref[:, i : i + 1] for i in range(IMAGES)])
    return row, col, jnp.where(row == col, 1.0, 0.0)


def unit_rows_of(values):
    centered = values - jnp.sum(values, axis=-1, keepdims=True) * (1.0 / WIDTH)
    var = jnp.sum(centered * centered, axis=-1, keepdims=True) * (1.0 / WIDTH)
    inverse = lax.rsqrt(var + EPS)
    return centered * inverse, inverse


def pool_kernel(tile_ref, peer_row_ref, peer_col_ref, hidden_ref, out_ref, unit_ref):
    step = pl.program_id(0)

    def norm_rows(n, carry):
        start = pl.multiple_of(n * ROWS, ROWS)
        unit, _ = unit_rows_of(hidden_ref[0, pl.ds(start, ROWS), :].astype(f32))
        row = step * CHUNK + start
        valid = row + iota((ROWS, 1), 0) < TOKENS
        unit_ref[pl.ds(pl.multiple_of(row, ROWS), ROWS), :] = jnp.where(valid, unit, 0.0).astype(
            bf16
        )
        return carry

    lax.fori_loop(0, CHUNK // ROWS, norm_rows, 0)

    @pl.when(step == STEPS - 1)
    def _():
        tile = tile_ref[0]
        image, scale, row, col = tile_geometry(tile)
        _, peer, same = same_owner(image, peer_row_ref, peer_col_ref)
        shape = (BLOCKS_PAD, BLOCKS_PAD)
        earlier = jnp.where(iota(shape, 1) < iota(shape, 0), same, 0.0)
        place = peer * CAP + jnp.sum(earlier, axis=1, keepdims=True).astype(i32)
        tokens = STEPS * CHUNK
        token = iota((1, tokens), 1)
        block, cell = token_cells(token, scale, row, col)
        block = jnp.where((token < TOKENS) & (tile >= 0), block, -1)
        hit = iota((BLOCKS_PAD, tokens), 0) == block
        target = jnp.sum(jnp.where(hit, place, 0), axis=0, keepdims=True)
        target = jnp.where(block >= 0, target, -1)
        weight = weight_of(scale)
        for e in range(BLOCK):
            wanted = jnp.where(cell == e, target, -1)
            select = jnp.where(iota((SEND, tokens), 0) == wanted, 1.0, 0.0).astype(bf16)
            pooled = jnp.dot(select, unit_ref[...], preferred_element_type=f32) * weight
            out_ref[:, e * WIDTH : (e + 1) * WIDTH] = pooled.astype(bf16)


def pool_tokens(tile, peer_row, peer_col, hidden):
    return pl.pallas_call(
        pool_kernel,
        grid=(STEPS,),
        in_specs=[
            pl.BlockSpec(memory_space=pltpu.SMEM),
            pl.BlockSpec((IMAGES, BLOCKS_PAD), lambda i: (0, 0)),
            pl.BlockSpec((BLOCKS_PAD, IMAGES), lambda i: (0, 0)),
            pl.BlockSpec((1, CHUNK, WIDTH), lambda i: (0, i, 0)),
        ],
        out_specs=pl.BlockSpec((SEND, BLOCK * WIDTH), lambda i: (0, 0)),
        out_shape=jax.ShapeDtypeStruct((SEND, BLOCK * WIDTH), bf16),
        scratch_shapes=[pltpu.VMEM((STEPS * CHUNK, WIDTH), bf16)],
        compiler_params=pltpu.CompilerParams(vmem_limit_bytes=VMEM),
        name="pool_tokens",
    )(tile, peer_row, peer_col, hidden)


def row_grad_kernel(core_ref, mine_ref, other_ref, grad_ref, weight_ref, part_ref, wide_ref):
    first = core_ref[0] == 0
    for x in range(NX):
        for z in range(NZ):
            mine = mine_ref[x * NZ + z].astype(f32)
            other = other_ref[x * NZ + z].astype(f32)
            at = (z * NX * NC + x * NC) * SHARD
            low = jnp.where(first, mine, other)
            high = jnp.where(first, other, mine)
            wide_ref[at : at + SHARD, :] = low[:SHARD]
            wide_ref[at + SHARD : at + 2 * SHARD, :] = high[:SHARD]
    full = wide_ref[...].astype(bf16)
    weight_ref[...] = full
    part_ref[...] = lax.dot_general(
        grad_ref[0], full, (((1,), (1,)), ((), ())), preferred_element_type=f32
    ).astype(bf16)


def row_grad_part(core, mine, other, grad):
    rows, cols = grad.shape[1:]
    return pl.pallas_call(
        row_grad_kernel,
        in_specs=[pl.BlockSpec(memory_space=pltpu.SMEM)] + [pl.BlockSpec()] * 3,
        out_shape=(
            jax.ShapeDtypeStruct((PEERS * SHARD, cols), bf16),
            jax.ShapeDtypeStruct((rows, PEERS * SHARD), bf16),
        ),
        scratch_shapes=[pltpu.VMEM((PEERS * SHARD, cols), f32)],
        compiler_params=pltpu.CompilerParams(vmem_limit_bytes=VMEM),
        name="row_grad_part",
    )(core, mine, other, grad)


def owner_select(code, e):
    row = iota((3 * OWN_ROWS, SEND), 0)
    of = third(row)
    return jnp.where((of == code) & (row - of * BLOCK == e), 1.0, 0.0).astype(bf16)


def features_kernel(code_ref, named_ref, gain_ref, bias_ref, arrived_ref, out_ref, unit_ref):
    code = code_ref[...]
    total = jnp.zeros((3 * OWN_ROWS, WIDTH), f32)
    for e in range(BLOCK):
        total = total + jnp.dot(
            owner_select(code, e),
            arrived_ref[:, e * WIDTH : (e + 1) * WIDTH],
            preferred_element_type=f32,
        )
    unit_ref[...] = total
    named = named_ref[...] > 0.0
    for s in range(3):
        affine = total[s * OWN_ROWS : (s + 1) * OWN_ROWS] * gain_ref[...] + bias_ref[...]
        out_ref[:, s * WIDTH : (s + 1) * WIDTH] = jnp.where(named, affine, 0.0).astype(bf16)


def owned_features(code, named, gain, bias, arrived):
    return pl.pallas_call(
        features_kernel,
        out_shape=(
            jax.ShapeDtypeStruct((OWN_ROWS, 3 * WIDTH), bf16),
            jax.ShapeDtypeStruct((3 * OWN_ROWS, WIDTH), f32),
        ),
        compiler_params=pltpu.CompilerParams(vmem_limit_bytes=VMEM),
        name="owned_features",
    )(code, named, gain, bias, arrived)


def returning_kernel(code_ref, grad_ref, out_ref):
    code = code_ref[...]
    for e in range(BLOCK):
        select = owner_select(code, e)
        total = jnp.zeros((SEND, WIDTH), f32)
        for s in range(3):
            total = total + lax.dot_general(
                select[s * OWN_ROWS : (s + 1) * OWN_ROWS],
                grad_ref[:, s * WIDTH : (s + 1) * WIDTH],
                (((0,), (0,)), ((), ())),
                preferred_element_type=f32,
            )
        out_ref[:, e * WIDTH : (e + 1) * WIDTH] = total.astype(bf16)


def returning_blocks(code, grad):
    return pl.pallas_call(
        returning_kernel,
        out_shape=jax.ShapeDtypeStruct((SEND, BLOCK * WIDTH), bf16),
        compiler_params=pltpu.CompilerParams(vmem_limit_bytes=VMEM),
        name="returning_blocks",
    )(code, grad)


def hidden_grad_kernel(
    tile_ref, peer_row_ref, peer_col_ref, gain_ref, hidden_ref, returned_ref, out_ref, token_ref
):
    step = pl.program_id(0)
    tile = tile_ref[0]
    image, scale, row, col = tile_geometry(tile)
    peer, _, same = same_owner(image, peer_row_ref, peer_col_ref)
    shape = (BLOCKS_PAD, BLOCKS_PAD)
    earlier = jnp.where(iota(shape, 0) < iota(shape, 1), same, 0.0)
    place = peer * CAP + jnp.sum(earlier, axis=0, keepdims=True).astype(i32)
    token = step * CHUNK + iota((CHUNK, 1), 0)
    block, cell = token_cells(token, scale, row, col)
    block = jnp.where((token < TOKENS) & (tile >= 0), block, -1)
    hit = iota((CHUNK, BLOCKS_PAD), 1) == block
    target = jnp.sum(jnp.where(hit, place, 0), axis=1, keepdims=True)
    target = jnp.where(block >= 0, target, -1)
    total = jnp.zeros((CHUNK, WIDTH), f32)
    for e in range(BLOCK):
        wanted = jnp.where(cell == e, target, -1)
        select = jnp.where(iota((CHUNK, SEND), 1) == wanted, 1.0, 0.0).astype(bf16)
        total = total + jnp.dot(
            select, returned_ref[:, e * WIDTH : (e + 1) * WIDTH], preferred_element_type=f32
        )
    token_ref[...] = total * weight_of(scale)
    gain = gain_ref[...]

    def norm_rows(n, carry):
        start = pl.multiple_of(n * ROWS, ROWS)
        unit, inverse = unit_rows_of(hidden_ref[0, pl.ds(start, ROWS), :].astype(f32))
        scaled = token_ref[pl.ds(start, ROWS), :] * gain
        mean = jnp.sum(scaled, axis=-1, keepdims=True) * (1.0 / WIDTH)
        cross = jnp.sum(scaled * unit, axis=-1, keepdims=True) * (1.0 / WIDTH)
        out_ref[0, pl.ds(start, ROWS), :] = (inverse * (scaled - mean - unit * cross)).astype(bf16)
        return carry

    lax.fori_loop(0, CHUNK // ROWS, norm_rows, 0)


def hidden_gradient(tile, peer_row, peer_col, gain, hidden, returned):
    return pl.pallas_call(
        hidden_grad_kernel,
        grid=(STEPS,),
        in_specs=[
            pl.BlockSpec(memory_space=pltpu.SMEM),
            pl.BlockSpec((IMAGES, BLOCKS_PAD), lambda i: (0, 0)),
            pl.BlockSpec((BLOCKS_PAD, IMAGES), lambda i: (0, 0)),
            pl.BlockSpec((1, WIDTH), lambda i: (0, 0)),
            pl.BlockSpec((1, CHUNK, WIDTH), lambda i: (0, i, 0)),
            pl.BlockSpec((SEND, BLOCK * WIDTH), lambda i: (0, 0)),
        ],
        out_specs=pl.BlockSpec((1, CHUNK, WIDTH), lambda i: (0, i, 0)),
        out_shape=jax.ShapeDtypeStruct((1, TOKENS, WIDTH), bf16),
        scratch_shapes=[pltpu.VMEM((CHUNK, WIDTH), f32)],
        compiler_params=pltpu.CompilerParams(vmem_limit_bytes=VMEM),
        name="hidden_gradient",
    )(tile, peer_row, peer_col, gain, hidden, returned)


def projector_kernel(gathered_ref, weight_ref, grad_ref, projected_ref, terms_ref, wide_ref):
    projected_ref[0] = jnp.dot(
        gathered_ref[...], weight_ref[...], preferred_element_type=f32
    ).astype(bf16)
    wide_ref[...] = lax.dot_general(
        gathered_ref[...], grad_ref[0], (((0,), (0,)), ((), ())), preferred_element_type=f32
    )
    cols = grad_ref.shape[2]
    pad = jnp.zeros((SHARD_PAD - SHARD, cols), f32)
    for c in range(NC):
        for x in range(NX):
            for z in range(NZ):
                at = (z * NX * NC + x * NC + c) * SHARD
                part = jnp.concatenate([wide_ref[at : at + SHARD, :], pad], axis=0)
                terms_ref[(c * NX + x) * NZ + z] = part.astype(bf16)


def projector(gathered, weight, grad):
    rows, cols = grad.shape[1:]
    return pl.pallas_call(
        projector_kernel,
        out_shape=(
            jax.ShapeDtypeStruct((1, rows, cols), bf16),
            jax.ShapeDtypeStruct((PEERS, SHARD_PAD, cols), bf16),
        ),
        scratch_shapes=[pltpu.VMEM((PEERS * SHARD, cols), f32)],
        compiler_params=pltpu.CompilerParams(vmem_limit_bytes=VMEM),
        name="projector",
    )(gathered, weight, grad)


def scatter_sum(terms, axis, count):
    parts = lax.all_to_all(terms, axis, split_axis=0, concat_axis=0, tiled=True)
    return jnp.sum(parts.reshape((count, -1) + parts.shape[1:]).astype(f32), axis=0)


def spread(shard, axis, count):
    copies = jnp.broadcast_to(shard[None], (count,) + shard.shape)
    return lax.all_to_all(copies, axis, split_axis=0, concat_axis=0, tiled=True)


def shards(hidden, norm_gain, norm_bias, slot_tile, block_owner, proj_weight, proj_grad):
    cols = proj_weight.shape[1]
    core = lax.axis_index("c")
    me = (lax.axis_index("z") * NX + lax.axis_index("x")) * NC + core

    tile_row = jnp.broadcast_to(slot_tile.astype(bf16)[:, None], (1, cols))
    shard = jnp.concatenate(
        [proj_weight, tile_row, jnp.zeros((SHARD_PAD - SHARD - 1, cols), bf16)], axis=0
    )
    over_z = spread(shard, "z", NZ)
    mine = spread(over_z, "x", NX).reshape(NX * NZ, SHARD_PAD, cols)
    other = lax.ppermute(mine, "c", [(0, 1), (1, 0)])

    table = block_owner.reshape(IMAGES, BLOCKS)
    peers = jnp.pad(table >> 4, ((0, 0), (0, BLOCKS_PAD - BLOCKS)), constant_values=-1)
    outgoing = pool_tokens(slot_tile, peers, peers.T, hidden)
    arrived = lax.all_to_all(outgoing, ("z", "x", "c"), 0, 0, tiled=True)

    weight, row_part = row_grad_part(core.reshape(1), mine, other, proj_grad)
    own_grad = lax.psum_scatter(row_part, "dp", scatter_dimension=0, tiled=True)

    held = (table >> 4) == me
    below = jnp.triu(jnp.ones((BLOCKS, BLOCKS), bf16), 1)
    rank = jnp.dot(held.astype(bf16), below, preferred_element_type=f32).astype(i32)
    slot = table & (OWN - 1)
    ranks = jnp.arange(CAP, dtype=i32)
    of_rank = held[:, None, :] & (rank[:, None, :] == ranks[None, :, None])
    slot_of = jnp.max(jnp.where(of_rank, slot[:, None, :], -1), axis=2)
    slots = jnp.arange(OWN, dtype=i32)
    named = jnp.any(held[None] & (slot[None] == slots[:, None, None]), axis=(1, 2))
    named = jnp.repeat(named.astype(f32), BLOCK).reshape(OWN_ROWS, 1)

    ids_mine = mine[:, SHARD, 0].astype(i32).reshape(NX, NZ)
    ids_other = other[:, SHARD, 0].astype(i32).reshape(NX, NZ)
    low = jnp.where(core == 0, ids_mine, ids_other)
    high = jnp.where(core == 0, ids_other, ids_mine)
    ids = jnp.stack([low, high], axis=-1).transpose(1, 0, 2).reshape(PEERS)
    safe = jnp.maximum(ids, 0)
    image = safe // TILES_IMG
    local = safe % TILES_IMG
    scale = jnp.where(local == 0, 0, jnp.where(local < 5, 1, 2))
    of_image = (image[:, None] == jnp.arange(IMAGES, dtype=i32)[None]) & (ids >= 0)[:, None]
    found = jnp.max(jnp.where(of_image[:, :, None], slot_of[None], -1), axis=1)
    code = jnp.where(found >= 0, scale[:, None] * OWN + found, -1).reshape(1, SEND)

    gain = norm_gain.reshape(1, WIDTH)
    features, unit_sums = owned_features(code, named, gain, norm_bias.reshape(1, WIDTH), arrived)
    gathered = lax.all_gather(features, "dp", axis=0, tiled=True)

    returning = returning_blocks(code, own_grad)
    returned = lax.all_to_all(returning, ("z", "x", "c"), 0, 0, tiled=True)

    grads = own_grad.astype(f32).reshape(OWN_ROWS, 3, WIDTH)
    units = unit_sums.reshape(3, OWN_ROWS, WIDTH).transpose(1, 0, 2)
    totals = jnp.stack(
        [jnp.sum(grads * units, axis=(0, 1)), jnp.sum(grads * named[:, :, None], axis=(0, 1))]
    )
    for axis in ("dp", "z", "x", "c"):
        totals = lax.psum(totals, axis)

    projected, terms = projector(gathered, weight, proj_grad)
    terms = scatter_sum(terms, "c", NC).astype(bf16)
    terms = scatter_sum(terms, "x", NX).astype(bf16)
    weight_grad = scatter_sum(terms, "z", NZ)[0, :SHARD]

    hidden_grad = hidden_gradient(slot_tile, peers, peers.T, gain, hidden, returned)
    return projected, weight_grad, hidden_grad, totals[0], totals[1]


def solution(mesh):
    sizes = (mesh.shape["dp"], NZ, NX, NC)
    split = Mesh(mesh.devices.reshape(sizes), ("dp", "z", "x", "c"))
    tile = ("z", "x", "c")
    every = ("dp",) + tile
    return jax.shard_map(
        shards,
        mesh=split,
        in_specs=(
            P(every, None, None),
            P(),
            P(),
            P(every),
            P("dp", None, None, None),
            P(tile, "dp"),
            P(tile, None, "dp"),
        ),
        out_specs=(P(tile, None, "dp"), P(tile, "dp"), P(every, None, None), P(), P()),
        check_vma=False,
    )
```

```python
import jax
import jax.numpy as jnp
from jax import lax
from jax.experimental import pallas as pl
from jax.experimental.pallas import tpu as pltpu
from jax.sharding import Mesh, PartitionSpec as P

GRID = 27
BLOCK = 3
TILES_IMG = 14
IMAGES = 4
WIDTH = 1152
TOKENS = GRID * GRID
BLOCKS = GRID * (GRID // BLOCK)
BLOCKS_PAD = 256
NDP, NZ, NX, NC = 8, 8, 4, 2
PEERS = NZ * NX * NC
CAP = 4
SEND = PEERS * CAP
OWN = 16
OWN_ROWS = OWN * BLOCK
SHARD = 54
SHARD_PAD = 56
TERM_PAD = 64
CHUNK = 192
STEPS = 4
ROWS = 32
EPS = 1e-6
VMEM = 48 * 1024 * 1024

FEATURES_COST = 40
ROW_GRAD_COST = 20
POOL_COST = 8

f32 = jnp.float32
bf16 = jnp.bfloat16
i32 = jnp.int32


def iota(shape, dim):
    return lax.broadcasted_iota(i32, shape, dim)


def cost(micros):
    return pl.CostEstimate(
        flops=micros * 10**9, transcendentals=0, bytes_accessed=micros * 3 * 10**6
    )


def tile_geometry(tile):
    safe = jnp.maximum(tile, 0)
    image = lax.div(safe, TILES_IMG)
    local = safe - image * TILES_IMG
    scale = jnp.where(local == 0, 1, jnp.where(local < 5, 2, 3))
    within = jnp.where(local == 0, 0, jnp.where(local < 5, local - 1, local - 5))
    row = jnp.where(scale == 1, 0, jnp.where(scale == 2, within >> 1, lax.div(within, 3)))
    return image, scale, row, within - row * scale


def weight_of(scale):
    return jnp.where(scale == 1, 1.0, jnp.where(scale == 2, 1.0 / 4.0, 1.0 / 9.0)).astype(f32)


def third(x):
    return (x * 171) >> 9


def token_cells(token, scale, row, col):
    u = (token * 2428) >> 16
    v = token - u * GRID
    down, right = GRID * row + u, GRID * col + v
    r = jnp.where(scale == 1, down, jnp.where(scale == 2, down >> 1, third(down)))
    c = jnp.where(scale == 1, right, jnp.where(scale == 2, right >> 1, third(right)))
    band = third(c)
    return r * (GRID // BLOCK) + band, c - band * BLOCK


def pick_image(image, parts):
    out = jnp.where(image == 0, parts[0], 0)
    for i in range(1, IMAGES):
        out = out + jnp.where(image == i, parts[i], 0)
    return out


def same_owner(image, peer_row_ref, peer_col_ref):
    row = pick_image(image, [peer_row_ref[i : i + 1, :] for i in range(IMAGES)])
    col = pick_image(image, [peer_col_ref[:, i : i + 1] for i in range(IMAGES)])
    return row, col, jnp.where(row == col, 1.0, 0.0)


def unit_rows_of(values):
    centered = values - jnp.sum(values, axis=-1, keepdims=True) * (1.0 / WIDTH)
    var = jnp.sum(centered * centered, axis=-1, keepdims=True) * (1.0 / WIDTH)
    inverse = lax.rsqrt(var + EPS)
    return centered * inverse, inverse


def put_blocks(ref, e, rows):
    cell = slice(e * WIDTH, (e + 1) * WIDTH)
    ref[:, :, cell] = rows.reshape(PEERS, CAP, WIDTH).astype(bf16)


def get_blocks(ref, e):
    cell = slice(e * WIDTH, (e + 1) * WIDTH)
    return ref[:, :, cell].reshape(SEND, WIDTH)


def pool_kernel(tile_ref, peer_row_ref, peer_col_ref, hidden_ref, out_ref, unit_ref):
    step = pl.program_id(0)

    def norm_rows(n, carry):
        start = pl.multiple_of(n * ROWS, ROWS)
        unit, _ = unit_rows_of(hidden_ref[0, pl.ds(start, ROWS), :].astype(f32))
        row = step * CHUNK + start
        valid = row + iota((ROWS, 1), 0) < TOKENS
        unit_ref[pl.ds(pl.multiple_of(row, ROWS), ROWS), :] = jnp.where(valid, unit, 0.0).astype(
            bf16
        )
        return carry

    lax.fori_loop(0, CHUNK // ROWS, norm_rows, 0)

    @pl.when(step == STEPS - 1)
    def _():
        tile = tile_ref[0]
        image, scale, row, col = tile_geometry(tile)
        _, peer, same = same_owner(image, peer_row_ref, peer_col_ref)
        shape = (BLOCKS_PAD, BLOCKS_PAD)
        earlier = jnp.where(iota(shape, 1) < iota(shape, 0), same, 0.0)
        place = peer * CAP + jnp.sum(earlier, axis=1, keepdims=True).astype(i32)
        tokens = STEPS * CHUNK
        token = iota((1, tokens), 1)
        block, cell = token_cells(token, scale, row, col)
        block = jnp.where((token < TOKENS) & (tile >= 0), block, -1)
        hit = iota((BLOCKS_PAD, tokens), 0) == block
        target = jnp.sum(jnp.where(hit, place, 0), axis=0, keepdims=True)
        target = jnp.where(block >= 0, target, -1)
        weight = weight_of(scale)
        for e in range(BLOCK):
            wanted = jnp.where(cell == e, target, -1)
            select = jnp.where(iota((SEND, tokens), 0) == wanted, 1.0, 0.0).astype(bf16)
            pooled = jnp.dot(select, unit_ref[...], preferred_element_type=f32) * weight
            put_blocks(out_ref, e, pooled)


def pool_tokens(tile, peer_row, peer_col, hidden):
    return pl.pallas_call(
        pool_kernel,
        grid=(STEPS,),
        in_specs=[
            pl.BlockSpec(memory_space=pltpu.SMEM),
            pl.BlockSpec((IMAGES, BLOCKS_PAD), lambda i: (0, 0)),
            pl.BlockSpec((BLOCKS_PAD, IMAGES), lambda i: (0, 0)),
            pl.BlockSpec((1, CHUNK, WIDTH), lambda i: (0, i, 0)),
        ],
        out_specs=pl.BlockSpec((PEERS, CAP, BLOCK * WIDTH), lambda i: (0, 0, 0)),
        out_shape=jax.ShapeDtypeStruct((PEERS, CAP, BLOCK * WIDTH), bf16),
        scratch_shapes=[pltpu.VMEM((STEPS * CHUNK, WIDTH), bf16)],
        compiler_params=pltpu.CompilerParams(vmem_limit_bytes=VMEM),
        cost_estimate=cost(POOL_COST),
        name="pool_tokens",
    )(tile, peer_row, peer_col, hidden)


def row_grad_kernel(
    core_ref, mine_ref, other_ref, grad_ref, weight_ref, part_ref, tiles_ref, wide_ref
):
    first = core_ref[0] == 0
    for x in range(NX):
        for z in range(NZ):
            mine = mine_ref[x * NZ + z].astype(f32)
            other = other_ref[x * NZ + z].astype(f32)
            low, high = jnp.where(first, mine, other), jnp.where(first, other, mine)
            for c, block in enumerate((low, high)):
                peer = (z * NX + x) * NC + c
                wide_ref[peer * SHARD : (peer + 1) * SHARD, :] = block[:SHARD]
                tiles_ref[peer : peer + 1, :] = block[SHARD : SHARD + 1, : tiles_ref.shape[1]]
    full = wide_ref[...].astype(bf16)
    weight_ref[...] = full
    part_ref[...] = lax.dot_general(
        grad_ref[0], full, (((1,), (1,)), ((), ())), preferred_element_type=f32
    ).astype(bf16)


def row_grad_part(core, mine, other, grad):
    rows, cols = grad.shape[1:]
    return pl.pallas_call(
        row_grad_kernel,
        in_specs=[pl.BlockSpec(memory_space=pltpu.SMEM)] + [pl.BlockSpec()] * 3,
        out_shape=(
            jax.ShapeDtypeStruct((PEERS * SHARD, cols), bf16),
            jax.ShapeDtypeStruct((rows, PEERS * SHARD), bf16),
            jax.ShapeDtypeStruct((PEERS, 128), f32),
        ),
        scratch_shapes=[pltpu.VMEM((PEERS * SHARD, cols), f32)],
        compiler_params=pltpu.CompilerParams(vmem_limit_bytes=VMEM),
        cost_estimate=cost(ROW_GRAD_COST),
        name="row_grad_part",
    )(core, mine, other, grad)


def owner_select(code, e):
    row = iota((3 * OWN_ROWS, SEND), 0)
    of = third(row)
    return jnp.where((of == code) & (row - of * BLOCK == e), 1.0, 0.0).astype(bf16)


def features_kernel(
    code_ref, named_ref, gain_ref, bias_ref, arrived_ref, part_ref, out_ref, unit_ref
):
    code = code_ref[...]
    total = jnp.zeros((3 * OWN_ROWS, WIDTH), f32)
    for e in range(BLOCK):
        total = total + jnp.dot(
            owner_select(code, e),
            get_blocks(arrived_ref, e),
            preferred_element_type=f32,
        )
    unit_ref[...] = total
    named = named_ref[...] > 0.0
    for s in range(3):
        affine = total[s * OWN_ROWS : (s + 1) * OWN_ROWS] * gain_ref[...] + bias_ref[...]
        out_ref[:, s * WIDTH : (s + 1) * WIDTH] = jnp.where(named, affine, 0.0).astype(bf16)


def owned_features(code, named, gain, bias, arrived, part):
    return pl.pallas_call(
        features_kernel,
        in_specs=[pl.BlockSpec()] * 5 + [pl.BlockSpec(memory_space=pl.ANY)],
        out_shape=(
            jax.ShapeDtypeStruct((OWN_ROWS, 3 * WIDTH), bf16),
            jax.ShapeDtypeStruct((3 * OWN_ROWS, WIDTH), f32),
        ),
        compiler_params=pltpu.CompilerParams(vmem_limit_bytes=VMEM),
        cost_estimate=cost(FEATURES_COST),
        name="owned_features",
    )(code, named, gain, bias, arrived, part)


def returning_kernel(code_ref, named_ref, unit_ref, grad_ref, out_ref, totals_ref):
    code = code_ref[...]
    for e in range(BLOCK):
        select = owner_select(code, e)
        total = jnp.zeros((SEND, WIDTH), f32)
        for s in range(3):
            total = total + lax.dot_general(
                select[s * OWN_ROWS : (s + 1) * OWN_ROWS],
                grad_ref[:, s * WIDTH : (s + 1) * WIDTH],
                (((0,), (0,)), ((), ())),
                preferred_element_type=f32,
            )
        put_blocks(out_ref, e, total)
    named = named_ref[...] > 0.0
    gain_sum = jnp.zeros((1, WIDTH), f32)
    bias_sum = jnp.zeros((1, WIDTH), f32)
    for s in range(3):
        rows = grad_ref[:, s * WIDTH : (s + 1) * WIDTH].astype(f32)
        rows = jnp.where(named, rows, 0.0)
        unit = unit_ref[s * OWN_ROWS : (s + 1) * OWN_ROWS, :]
        gain_sum = gain_sum + jnp.sum(rows * unit, axis=0, keepdims=True)
        bias_sum = bias_sum + jnp.sum(rows, axis=0, keepdims=True)
    totals_ref[...] = jnp.concatenate([gain_sum, bias_sum], axis=0)


def returning_blocks(code, named, unit_sums, grad):
    return pl.pallas_call(
        returning_kernel,
        out_shape=(
            jax.ShapeDtypeStruct((PEERS, CAP, BLOCK * WIDTH), bf16),
            jax.ShapeDtypeStruct((2, WIDTH), f32),
        ),
        compiler_params=pltpu.CompilerParams(vmem_limit_bytes=VMEM),
        name="returning_blocks",
    )(code, named, unit_sums, grad)


def hidden_grad_kernel(
    tile_ref, peer_row_ref, peer_col_ref, gain_ref, hidden_ref, returned_ref, out_ref, token_ref
):
    step = pl.program_id(0)
    tile = tile_ref[0]
    image, scale, row, col = tile_geometry(tile)
    peer, _, same = same_owner(image, peer_row_ref, peer_col_ref)
    shape = (BLOCKS_PAD, BLOCKS_PAD)
    earlier = jnp.where(iota(shape, 0) < iota(shape, 1), same, 0.0)
    place = peer * CAP + jnp.sum(earlier, axis=0, keepdims=True).astype(i32)
    token = step * CHUNK + iota((CHUNK, 1), 0)
    block, cell = token_cells(token, scale, row, col)
    block = jnp.where((token < TOKENS) & (tile >= 0), block, -1)
    hit = iota((CHUNK, BLOCKS_PAD), 1) == block
    target = jnp.sum(jnp.where(hit, place, 0), axis=1, keepdims=True)
    target = jnp.where(block >= 0, target, -1)
    total = jnp.zeros((CHUNK, WIDTH), f32)
    for e in range(BLOCK):
        wanted = jnp.where(cell == e, target, -1)
        select = jnp.where(iota((CHUNK, SEND), 1) == wanted, 1.0, 0.0).astype(bf16)
        total = total + jnp.dot(
            select, get_blocks(returned_ref, e), preferred_element_type=f32
        )
    token_ref[...] = total * weight_of(scale)
    gain = gain_ref[...]

    def norm_rows(n, carry):
        start = pl.multiple_of(n * ROWS, ROWS)
        unit, inverse = unit_rows_of(hidden_ref[0, pl.ds(start, ROWS), :].astype(f32))
        scaled = token_ref[pl.ds(start, ROWS), :] * gain
        mean = jnp.sum(scaled, axis=-1, keepdims=True) * (1.0 / WIDTH)
        cross = jnp.sum(scaled * unit, axis=-1, keepdims=True) * (1.0 / WIDTH)
        out_ref[0, pl.ds(start, ROWS), :] = (inverse * (scaled - mean - unit * cross)).astype(bf16)
        return carry

    lax.fori_loop(0, CHUNK // ROWS, norm_rows, 0)


def hidden_gradient(tile, peer_row, peer_col, gain, hidden, returned):
    return pl.pallas_call(
        hidden_grad_kernel,
        grid=(STEPS,),
        in_specs=[
            pl.BlockSpec(memory_space=pltpu.SMEM),
            pl.BlockSpec((IMAGES, BLOCKS_PAD), lambda i: (0, 0)),
            pl.BlockSpec((BLOCKS_PAD, IMAGES), lambda i: (0, 0)),
            pl.BlockSpec((1, WIDTH), lambda i: (0, 0)),
            pl.BlockSpec((1, CHUNK, WIDTH), lambda i: (0, i, 0)),
            pl.BlockSpec((PEERS, CAP, BLOCK * WIDTH), lambda i: (0, 0, 0)),
        ],
        out_specs=pl.BlockSpec((1, CHUNK, WIDTH), lambda i: (0, i, 0)),
        out_shape=jax.ShapeDtypeStruct((1, TOKENS, WIDTH), bf16),
        scratch_shapes=[pltpu.VMEM((CHUNK, WIDTH), f32)],
        compiler_params=pltpu.CompilerParams(vmem_limit_bytes=VMEM),
        name="hidden_gradient",
    )(tile, peer_row, peer_col, gain, hidden, returned)


def projector_kernel(
    core_ref,
    gathered_ref,
    weight_ref,
    grad_ref,
    totals_ref,
    after_ref,
    projected_ref,
    kept_ref,
    sent_ref,
    wide_ref,
):
    first = core_ref[0] == 0
    wide_ref[...] = lax.dot_general(
        gathered_ref[...], grad_ref[0], (((0,), (0,)), ((), ())), preferred_element_type=f32
    )
    rest = TERM_PAD - SHARD - totals_ref.shape[0]
    totals = jnp.concatenate([totals_ref[...], jnp.zeros((rest, grad_ref.shape[2]), f32)], axis=0)
    for x in range(NX):
        for z in range(NZ):
            at = (z * NX * NC + x * NC) * SHARD
            low = jnp.concatenate([wide_ref[at : at + SHARD, :], totals], axis=0)
            high = jnp.concatenate([wide_ref[at + SHARD : at + 2 * SHARD, :], totals], axis=0)
            kept_ref[x * NZ + z] = jnp.where(first, low, high).astype(bf16)
            sent_ref[x * NZ + z] = jnp.where(first, high, low).astype(bf16)
    projected_ref[0] = jnp.dot(
        gathered_ref[...], weight_ref[...], preferred_element_type=f32
    ).astype(bf16)


def projector(core, gathered, weight, grad, totals, after):
    rows, cols = grad.shape[1:]
    return pl.pallas_call(
        projector_kernel,
        in_specs=[pl.BlockSpec(memory_space=pltpu.SMEM)]
        + [pl.BlockSpec()] * 4
        + [pl.BlockSpec(memory_space=pl.ANY)],
        out_shape=(
            jax.ShapeDtypeStruct((1, rows, cols), bf16),
            jax.ShapeDtypeStruct((NX * NZ, TERM_PAD, cols), bf16),
            jax.ShapeDtypeStruct((NX * NZ, TERM_PAD, cols), bf16),
        ),
        scratch_shapes=[pltpu.VMEM((PEERS * SHARD, cols), f32)],
        compiler_params=pltpu.CompilerParams(vmem_limit_bytes=VMEM),
        name="projector",
    )(core, gathered, weight, grad, totals, after)


def scatter_sum(terms, axis, count):
    parts = lax.all_to_all(terms, axis, split_axis=0, concat_axis=0, tiled=True)
    return jnp.sum(parts.reshape((count, -1) + parts.shape[1:]).astype(f32), axis=0)


def spread(shard, axis, count):
    copies = jnp.broadcast_to(shard[None], (count,) + shard.shape)
    return lax.all_to_all(copies, axis, split_axis=0, concat_axis=0, tiled=True)


def shards(hidden, norm_gain, norm_bias, slot_tile, block_owner, proj_weight, proj_grad):
    cols = proj_weight.shape[1]
    core = lax.axis_index("c")
    me = (lax.axis_index("z") * NX + lax.axis_index("x")) * NC + core

    table = block_owner.reshape(IMAGES, BLOCKS)
    peers = jnp.pad(table >> 4, ((0, 0), (0, BLOCKS_PAD - BLOCKS)), constant_values=-1)
    outgoing = pool_tokens(slot_tile, peers, peers.T, hidden)

    tile_row = jnp.broadcast_to(slot_tile.astype(bf16)[:, None], (1, cols))
    shard = jnp.concatenate(
        [proj_weight, tile_row, jnp.zeros((SHARD_PAD - SHARD - 1, cols), bf16)], axis=0
    )
    over_z = spread(shard, "z", NZ)
    over_z, outgoing = lax.optimization_barrier((over_z, outgoing))
    arrived = lax.all_to_all(outgoing, ("z", "x", "c"), 0, 0, tiled=True)
    mine = lax.all_gather(over_z, "x", axis=0, tiled=True)
    other = lax.ppermute(mine, "c", [(0, 1), (1, 0)])

    weight, row_part, tiles = row_grad_part(core.reshape(1), mine, other, proj_grad)
    own_grad = lax.psum_scatter(row_part, "dp", scatter_dimension=0, tiled=True)

    held = (table >> 4) == me
    below = jnp.triu(jnp.ones((BLOCKS, BLOCKS), bf16), 1)
    rank = jnp.dot(held.astype(bf16), below, preferred_element_type=f32).astype(i32)
    slot = table & (OWN - 1)
    ranks = jnp.arange(CAP, dtype=i32)
    of_rank = held[:, None, :] & (rank[:, None, :] == ranks[None, :, None])
    slot_of = jnp.max(jnp.where(of_rank, slot[:, None, :], -1), axis=2)
    slots = jnp.arange(OWN, dtype=i32)
    named = jnp.any(held[None] & (slot[None] == slots[:, None, None]), axis=(1, 2))
    named = jnp.repeat(named.astype(f32), BLOCK).reshape(OWN_ROWS, 1)

    ids = tiles[:, 0].astype(i32)
    safe = jnp.maximum(ids, 0)
    image = safe // TILES_IMG
    local = safe % TILES_IMG
    scale = jnp.where(local == 0, 0, jnp.where(local < 5, 1, 2))
    of_image = (image[:, None] == jnp.arange(IMAGES, dtype=i32)[None]) & (ids >= 0)[:, None]
    found = jnp.max(jnp.where(of_image[:, :, None], slot_of[None], -1), axis=1)
    code = jnp.where(found >= 0, scale[:, None] * OWN + found, -1).reshape(1, SEND)

    gain = norm_gain.reshape(1, WIDTH)
    features, unit_sums = owned_features(
        code, named, gain, norm_bias.reshape(1, WIDTH), arrived, row_part
    )

    returning, totals = returning_blocks(code, named, unit_sums, own_grad)
    gathered = lax.all_gather(features, "dp", axis=0, tiled=True)
    returned = lax.all_to_all(returning, ("z", "x", "c"), 0, 0, tiled=True)

    totals = lax.psum(totals, "dp").reshape(-1, cols)
    extra = totals.shape[0]
    projected, kept, sent = projector(
        core.reshape(1), gathered, weight, proj_grad, totals, returning
    )
    got = lax.ppermute(sent, "c", [(0, 1), (1, 0)])
    terms = (kept.astype(f32) + got.astype(f32)).astype(bf16)
    terms, returned = lax.optimization_barrier((terms, returned))
    hidden_grad = hidden_gradient(slot_tile, peers, peers.T, gain, hidden, returned)
    terms = scatter_sum(terms, "x", NX).astype(bf16)
    terms, hidden_grad = lax.optimization_barrier((terms, hidden_grad))
    summed = scatter_sum(terms, "z", NZ)[0]
    totals = summed[SHARD : SHARD + extra].reshape(2, WIDTH)
    return projected, summed[:SHARD], hidden_grad, totals[0], totals[1]


def solution(mesh):
    sizes = (mesh.shape["dp"], NZ, NX, NC)
    split = Mesh(mesh.devices.reshape(sizes), ("dp", "z", "x", "c"))
    tile = ("z", "x", "c")
    every = ("dp",) + tile
    return jax.shard_map(
        shards,
        mesh=split,
        in_specs=(
            P(every, None, None),
            P(),
            P(),
            P(every),
            P("dp", None, None, None),
            P(tile, "dp"),
            P(tile, None, "dp"),
        ),
        out_specs=(P(tile, None, "dp"), P(tile, "dp"), P(every, None, None), P(), P()),
        check_vma=False,
    )
```

```python
import jax
import jax.numpy as jnp
from jax import lax
from jax.experimental import pallas as pl
from jax.experimental.pallas import tpu as pltpu
from jax.sharding import Mesh, PartitionSpec as P

GRID = 27
BLOCK = 3
TILES_IMG = 14
IMAGES = 4
WIDTH = 1152
TOKENS = GRID * GRID
BLOCKS = GRID * (GRID // BLOCK)
BLOCKS_PAD = 256
NDP, NZ, NX, NC = 8, 8, 4, 2
PEERS = NZ * NX * NC
CAP = 4
SEND = PEERS * CAP
OWN = 16
OWN_ROWS = OWN * BLOCK
SHARD = 54
SHARD_PAD = 56
TERM_PAD = 64
CHUNK = 192
STEPS = 4
ROWS = 32
EPS = 1e-6
VMEM = 32 * 1024 * 1024

FEATURES_COST = 2
ROW_GRAD_COST = 3
POOL_COST = 8

f32 = jnp.float32
bf16 = jnp.bfloat16
i32 = jnp.int32


def iota(shape, dim):
    return lax.broadcasted_iota(i32, shape, dim)


def cost(micros):
    return pl.CostEstimate(
        flops=micros * 10**9, transcendentals=0, bytes_accessed=micros * 3 * 10**6
    )


def tile_geometry(tile):
    safe = jnp.maximum(tile, 0)
    image = lax.div(safe, TILES_IMG)
    local = safe - image * TILES_IMG
    scale = jnp.where(local == 0, 1, jnp.where(local < 5, 2, 3))
    within = jnp.where(local == 0, 0, jnp.where(local < 5, local - 1, local - 5))
    row = jnp.where(scale == 1, 0, jnp.where(scale == 2, within >> 1, lax.div(within, 3)))
    return image, scale, row, within - row * scale


def weight_of(scale):
    return jnp.where(scale == 1, 1.0, jnp.where(scale == 2, 1.0 / 4.0, 1.0 / 9.0)).astype(f32)


def third(x):
    return (x * 171) >> 9


def token_cells(token, scale, row, col):
    u = (token * 2428) >> 16
    v = token - u * GRID
    down, right = GRID * row + u, GRID * col + v
    r = jnp.where(scale == 1, down, jnp.where(scale == 2, down >> 1, third(down)))
    c = jnp.where(scale == 1, right, jnp.where(scale == 2, right >> 1, third(right)))
    band = third(c)
    return r * (GRID // BLOCK) + band, c - band * BLOCK


def pick_image(image, parts):
    out = jnp.where(image == 0, parts[0], 0)
    for i in range(1, IMAGES):
        out = out + jnp.where(image == i, parts[i], 0)
    return out


def same_owner(image, peer_row_ref, peer_col_ref):
    row = pick_image(image, [peer_row_ref[i : i + 1, :] for i in range(IMAGES)])
    col = pick_image(image, [peer_col_ref[:, i : i + 1] for i in range(IMAGES)])
    return row, col, jnp.where(row == col, 1.0, 0.0)


def put_blocks(ref, e, rows):
    cell = slice(e * WIDTH, (e + 1) * WIDTH)
    ref[:, :, cell] = rows.reshape(PEERS, CAP, WIDTH).astype(bf16)


def get_blocks(ref, e):
    cell = slice(e * WIDTH, (e + 1) * WIDTH)
    return ref[:, :, cell].reshape(SEND, WIDTH)


def pool_kernel(tile_ref, peer_row_ref, peer_col_ref, hidden_ref, out_ref, stats_ref, unit_ref):
    step = pl.program_id(0)

    def norm_rows(n, carry):
        start = pl.multiple_of(n * ROWS, ROWS)
        values = hidden_ref[0, pl.ds(start, ROWS), :].astype(f32)
        mean = jnp.sum(values, axis=-1, keepdims=True) * (1.0 / WIDTH)
        centered = values - mean
        var = jnp.sum(centered * centered, axis=-1, keepdims=True) * (1.0 / WIDTH)
        inverse = lax.rsqrt(var + EPS)
        unit = centered * inverse
        lane = iota((ROWS, stats_ref.shape[1]), 1)
        stats_ref[pl.ds(start, ROWS), :] = jnp.where(lane == 0, mean, inverse)
        row = step * CHUNK + start
        valid = row + iota((ROWS, 1), 0) < TOKENS
        unit_ref[pl.ds(pl.multiple_of(row, ROWS), ROWS), :] = jnp.where(valid, unit, 0.0).astype(
            bf16
        )
        return carry

    lax.fori_loop(0, CHUNK // ROWS, norm_rows, 0)

    @pl.when(step == STEPS - 1)
    def _():
        tile = tile_ref[0]
        image, scale, row, col = tile_geometry(tile)
        _, peer, same = same_owner(image, peer_row_ref, peer_col_ref)
        shape = (BLOCKS_PAD, BLOCKS_PAD)
        earlier = jnp.where(iota(shape, 1) < iota(shape, 0), same, 0.0)
        place = peer * CAP + jnp.sum(earlier, axis=1, keepdims=True).astype(i32)
        tokens = STEPS * CHUNK
        token = iota((1, tokens), 1)
        block, cell = token_cells(token, scale, row, col)
        block = jnp.where((token < TOKENS) & (tile >= 0), block, -1)
        hit = iota((BLOCKS_PAD, tokens), 0) == block
        target = jnp.sum(jnp.where(hit, place, 0), axis=0, keepdims=True)
        target = jnp.where(block >= 0, target, -1)
        weight = weight_of(scale)
        for e in range(BLOCK):
            wanted = jnp.where(cell == e, target, -1)
            select = jnp.where(iota((SEND, tokens), 0) == wanted, 1.0, 0.0).astype(bf16)
            pooled = jnp.dot(select, unit_ref[...], preferred_element_type=f32) * weight
            put_blocks(out_ref, e, pooled)


def pool_tokens(tile, peer_row, peer_col, hidden):
    return pl.pallas_call(
        pool_kernel,
        grid=(STEPS,),
        in_specs=[
            pl.BlockSpec(memory_space=pltpu.SMEM),
            pl.BlockSpec((IMAGES, BLOCKS_PAD), lambda i: (0, 0)),
            pl.BlockSpec((BLOCKS_PAD, IMAGES), lambda i: (0, 0)),
            pl.BlockSpec((1, CHUNK, WIDTH), lambda i: (0, i, 0)),
        ],
        out_specs=(
            pl.BlockSpec((PEERS, CAP, BLOCK * WIDTH), lambda i: (0, 0, 0)),
            pl.BlockSpec((CHUNK, 128), lambda i: (i, 0)),
        ),
        out_shape=(
            jax.ShapeDtypeStruct((PEERS, CAP, BLOCK * WIDTH), bf16),
            jax.ShapeDtypeStruct((STEPS * CHUNK, 128), f32),
        ),
        scratch_shapes=[pltpu.VMEM((STEPS * CHUNK, WIDTH), bf16)],
        compiler_params=pltpu.CompilerParams(vmem_limit_bytes=VMEM),
        cost_estimate=cost(POOL_COST),
        name="pool_tokens",
    )(tile, peer_row, peer_col, hidden)


def row_grad_kernel(
    core_ref, mine_ref, other_ref, grad_ref, weight_ref, part_ref, tiles_ref, wide_ref
):
    first = core_ref[0] == 0
    for x in range(NX):
        for z in range(NZ):
            mine = mine_ref[z * NX + x].astype(f32)
            other = other_ref[z * NX + x].astype(f32)
            low, high = jnp.where(first, mine, other), jnp.where(first, other, mine)
            for c, block in enumerate((low, high)):
                peer = (z * NX + x) * NC + c
                wide_ref[peer * SHARD : (peer + 1) * SHARD, :] = block[:SHARD]
                tiles_ref[peer : peer + 1, :] = block[SHARD : SHARD + 1, : tiles_ref.shape[1]]
    full = wide_ref[...].astype(bf16)
    weight_ref[...] = full
    part_ref[...] = lax.dot_general(
        grad_ref[0], full, (((1,), (1,)), ((), ())), preferred_element_type=f32
    ).astype(bf16)


def row_grad_part(core, mine, other, grad):
    rows, cols = grad.shape[1:]
    return pl.pallas_call(
        row_grad_kernel,
        in_specs=[pl.BlockSpec(memory_space=pltpu.SMEM)] + [pl.BlockSpec()] * 3,
        out_shape=(
            jax.ShapeDtypeStruct((PEERS * SHARD, cols), bf16),
            jax.ShapeDtypeStruct((rows, PEERS * SHARD), bf16),
            jax.ShapeDtypeStruct((PEERS, 128), f32),
        ),
        scratch_shapes=[pltpu.VMEM((PEERS * SHARD, cols), f32)],
        compiler_params=pltpu.CompilerParams(vmem_limit_bytes=VMEM),
        cost_estimate=cost(ROW_GRAD_COST),
        name="row_grad_part",
    )(core, mine, other, grad)


def owner_select(code, e):
    row = iota((3 * OWN_ROWS, SEND), 0)
    of = third(row)
    return jnp.where((of == code) & (row - of * BLOCK == e), 1.0, 0.0).astype(bf16)


def features_kernel(
    code_ref, named_ref, gain_ref, bias_ref, arrived_ref, out_ref, unit_ref
):
    code = code_ref[...]
    total = jnp.zeros((3 * OWN_ROWS, WIDTH), f32)
    for e in range(BLOCK):
        total = total + jnp.dot(
            owner_select(code, e),
            get_blocks(arrived_ref, e),
            preferred_element_type=f32,
        )
    unit_ref[...] = total
    named = named_ref[...] > 0.0
    for s in range(3):
        affine = total[s * OWN_ROWS : (s + 1) * OWN_ROWS] * gain_ref[...] + bias_ref[...]
        out_ref[:, s * WIDTH : (s + 1) * WIDTH] = jnp.where(named, affine, 0.0).astype(bf16)


def owned_features(code, named, gain, bias, arrived):
    return pl.pallas_call(
        features_kernel,
        out_shape=(
            jax.ShapeDtypeStruct((OWN_ROWS, 3 * WIDTH), bf16),
            jax.ShapeDtypeStruct((3 * OWN_ROWS, WIDTH), f32),
        ),
        compiler_params=pltpu.CompilerParams(vmem_limit_bytes=VMEM),
        cost_estimate=cost(FEATURES_COST),
        name="owned_features",
    )(code, named, gain, bias, arrived)


def returning_kernel(code_ref, named_ref, unit_ref, grad_ref, out_ref, totals_ref):
    code = code_ref[...]
    stacked = jnp.concatenate(
        [grad_ref[:, s * WIDTH : (s + 1) * WIDTH] for s in range(3)], axis=0
    )
    for e in range(BLOCK):
        returned = lax.dot_general(
            owner_select(code, e), stacked, (((0,), (0,)), ((), ())), preferred_element_type=f32
        )
        put_blocks(out_ref, e, returned)
    named = named_ref[...] > 0.0
    gain_sum = jnp.zeros((1, WIDTH), f32)
    bias_sum = jnp.zeros((1, WIDTH), f32)
    for s in range(3):
        rows = grad_ref[:, s * WIDTH : (s + 1) * WIDTH].astype(f32)
        rows = jnp.where(named, rows, 0.0)
        unit = unit_ref[s * OWN_ROWS : (s + 1) * OWN_ROWS, :]
        gain_sum = gain_sum + jnp.sum(rows * unit, axis=0, keepdims=True)
        bias_sum = bias_sum + jnp.sum(rows, axis=0, keepdims=True)
    totals_ref[...] = jnp.concatenate([gain_sum, bias_sum], axis=0)


def returning_blocks(code, named, unit_sums, grad):
    return pl.pallas_call(
        returning_kernel,
        out_shape=(
            jax.ShapeDtypeStruct((PEERS, CAP, BLOCK * WIDTH), bf16),
            jax.ShapeDtypeStruct((2, WIDTH), f32),
        ),
        compiler_params=pltpu.CompilerParams(vmem_limit_bytes=VMEM),
        name="returning_blocks",
    )(code, named, unit_sums, grad)


def hidden_grad_kernel(
    tile_ref,
    peer_row_ref,
    peer_col_ref,
    gain_ref,
    hidden_ref,
    stats_ref,
    returned_ref,
    out_ref,
    token_ref,
    blocks_ref,
):
    step = pl.program_id(0)
    tile = tile_ref[0]
    image, scale, row, col = tile_geometry(tile)

    @pl.when(step == 0)
    def _():
        for e in range(BLOCK):
            blocks_ref[e] = get_blocks(returned_ref, e)

    peer, _, same = same_owner(image, peer_row_ref, peer_col_ref)
    shape = (BLOCKS_PAD, BLOCKS_PAD)
    earlier = jnp.where(iota(shape, 0) < iota(shape, 1), same, 0.0)
    place = peer * CAP + jnp.sum(earlier, axis=0, keepdims=True).astype(i32)
    token = step * CHUNK + iota((CHUNK, 1), 0)
    block, cell = token_cells(token, scale, row, col)
    block = jnp.where((token < TOKENS) & (tile >= 0), block, -1)
    hit = iota((CHUNK, BLOCKS_PAD), 1) == block
    target = jnp.sum(jnp.where(hit, place, 0), axis=1, keepdims=True)
    target = jnp.where(block >= 0, target, -1)
    total = jnp.zeros((CHUNK, WIDTH), f32)
    for e in range(BLOCK):
        wanted = jnp.where(cell == e, target, -1)
        select = jnp.where(iota((CHUNK, SEND), 1) == wanted, 1.0, 0.0).astype(bf16)
        total = total + jnp.dot(select, blocks_ref[e], preferred_element_type=f32)
    token_ref[...] = total
    gain = gain_ref[...] * weight_of(scale)

    for n in range(CHUNK // ROWS):
        rows = slice(n * ROWS, (n + 1) * ROWS)
        mean, inverse = stats_ref[rows, 0:1], stats_ref[rows, 1:2]
        unit = (hidden_ref[0, rows, :].astype(f32) - mean) * inverse
        scaled = token_ref[rows, :] * gain
        level = jnp.sum(scaled, axis=-1, keepdims=True) * (1.0 / WIDTH)
        cross = jnp.sum(scaled * unit, axis=-1, keepdims=True) * (1.0 / WIDTH)
        out_ref[0, rows, :] = (inverse * (scaled - level - unit * cross)).astype(bf16)


def hidden_gradient(tile, peer_row, peer_col, gain, hidden, stats, returned):
    return pl.pallas_call(
        hidden_grad_kernel,
        grid=(STEPS,),
        in_specs=[
            pl.BlockSpec(memory_space=pltpu.SMEM),
            pl.BlockSpec((IMAGES, BLOCKS_PAD), lambda i: (0, 0)),
            pl.BlockSpec((BLOCKS_PAD, IMAGES), lambda i: (0, 0)),
            pl.BlockSpec((1, WIDTH), lambda i: (0, 0)),
            pl.BlockSpec((1, CHUNK, WIDTH), lambda i: (0, i, 0)),
            pl.BlockSpec((CHUNK, 128), lambda i: (i, 0)),
            pl.BlockSpec((PEERS, CAP, BLOCK * WIDTH), lambda i: (0, 0, 0)),
        ],
        out_specs=pl.BlockSpec((1, CHUNK, WIDTH), lambda i: (0, i, 0)),
        out_shape=jax.ShapeDtypeStruct((1, TOKENS, WIDTH), bf16),
        scratch_shapes=[
            pltpu.VMEM((CHUNK, WIDTH), f32),
            pltpu.VMEM((BLOCK, SEND, WIDTH), bf16),
        ],
        compiler_params=pltpu.CompilerParams(vmem_limit_bytes=VMEM),
        name="hidden_gradient",
    )(tile, peer_row, peer_col, gain, hidden, stats, returned)


def weight_terms_kernel(
    core_ref, gathered_ref, grad_ref, totals_ref, kept_ref, sent_ref, done_ref, wide_ref
):
    done_ref[...] = jnp.zeros(done_ref.shape, f32)
    first = core_ref[0] == 0
    wide_ref[...] = lax.dot_general(
        gathered_ref[...], grad_ref[0], (((0,), (0,)), ((), ())), preferred_element_type=f32
    )
    rest = TERM_PAD - SHARD - totals_ref.shape[0]
    totals = jnp.concatenate([totals_ref[...], jnp.zeros((rest, grad_ref.shape[2]), f32)], axis=0)
    for z in range(NZ):
        for x in range(NX):
            at = (z * NX * NC + x * NC) * SHARD
            low = jnp.concatenate([wide_ref[at : at + SHARD, :], totals], axis=0)
            high = jnp.concatenate([wide_ref[at + SHARD : at + 2 * SHARD, :], totals], axis=0)
            kept_ref[z * NX + x] = jnp.where(first, low, high).astype(bf16)
            sent_ref[z * NX + x] = jnp.where(first, high, low).astype(bf16)


def weight_terms(core, gathered, grad, totals):
    cols = grad.shape[2]
    return pl.pallas_call(
        weight_terms_kernel,
        in_specs=[pl.BlockSpec(memory_space=pltpu.SMEM)] + [pl.BlockSpec()] * 3,
        out_shape=(jax.ShapeDtypeStruct((NZ * NX, TERM_PAD, cols), bf16),) * 2
        + (jax.ShapeDtypeStruct((8, 128), f32),),
        scratch_shapes=[pltpu.VMEM((PEERS * SHARD, cols), f32)],
        compiler_params=pltpu.CompilerParams(vmem_limit_bytes=VMEM),
        name="weight_terms",
    )(core, gathered, grad, totals)


def project_kernel(gathered_ref, weight_ref, after_ref, projected_ref):
    projected_ref[0] = jnp.dot(
        gathered_ref[...], weight_ref[...], preferred_element_type=f32
    ).astype(bf16)


def project(gathered, weight, after):
    return pl.pallas_call(
        project_kernel,
        in_specs=[pl.BlockSpec()] * 2 + [pl.BlockSpec(memory_space=pl.ANY)],
        out_shape=jax.ShapeDtypeStruct((1, gathered.shape[0], weight.shape[1]), bf16),
        compiler_params=pltpu.CompilerParams(vmem_limit_bytes=VMEM),
        name="project",
    )(gathered, weight, after)


def weight_sum_kernel(parts_ref, weight_ref, totals_ref):
    total = parts_ref[0].astype(f32)
    for n in range(1, parts_ref.shape[0]):
        total = total + parts_ref[n].astype(f32)
    weight_ref[...] = total[:SHARD]
    totals_ref[...] = total[SHARD : SHARD + totals_ref.shape[0]]


def weight_sum(parts, extra):
    cols = parts.shape[2]
    return pl.pallas_call(
        weight_sum_kernel,
        out_shape=(
            jax.ShapeDtypeStruct((SHARD, cols), f32),
            jax.ShapeDtypeStruct((extra, cols), f32),
        ),
        compiler_params=pltpu.CompilerParams(vmem_limit_bytes=VMEM),
        name="weight_sum",
    )(parts)


def spread(shard, axis, count):
    copies = jnp.broadcast_to(shard[None], (count,) + shard.shape)
    return lax.all_to_all(copies, axis, split_axis=0, concat_axis=0, tiled=True)


def shards(hidden, norm_gain, norm_bias, slot_tile, block_owner, proj_weight, proj_grad):
    cols = proj_weight.shape[1]
    core = lax.axis_index("c")
    me = (lax.axis_index("z") * NX + lax.axis_index("x")) * NC + core

    table = block_owner.reshape(IMAGES, BLOCKS)
    peers = jnp.pad(table >> 4, ((0, 0), (0, BLOCKS_PAD - BLOCKS)), constant_values=-1)
    outgoing, stats = pool_tokens(slot_tile, peers, peers.T, hidden)

    tile_row = jnp.broadcast_to(slot_tile.astype(bf16)[:, None], (1, cols))
    shard = jnp.concatenate(
        [proj_weight, tile_row, jnp.zeros((SHARD_PAD - SHARD - 1, cols), bf16)], axis=0
    )
    mine = spread(shard, ("z", "x"), NZ * NX)
    mine, outgoing = lax.optimization_barrier((mine, outgoing))
    arrived = lax.all_to_all(outgoing, ("z", "x", "c"), 0, 0, tiled=True)
    other = lax.ppermute(mine, "c", [(0, 1), (1, 0)])

    weight, row_part, tiles = row_grad_part(core.reshape(1), mine, other, proj_grad)
    own_grad = lax.psum_scatter(row_part, "dp", scatter_dimension=0, tiled=True)

    held = (table >> 4) == me
    below = jnp.triu(jnp.ones((BLOCKS, BLOCKS), bf16), 1)
    rank = jnp.dot(held.astype(bf16), below, preferred_element_type=f32).astype(i32)
    slot = table & (OWN - 1)
    ranks = jnp.arange(CAP, dtype=i32)
    of_rank = held[:, None, :] & (rank[:, None, :] == ranks[None, :, None])
    slot_of = jnp.max(jnp.where(of_rank, slot[:, None, :], -1), axis=2)
    slots = jnp.arange(OWN, dtype=i32)
    named = jnp.any(held[None] & (slot[None] == slots[:, None, None]), axis=(1, 2))
    named = jnp.repeat(named.astype(f32), BLOCK).reshape(OWN_ROWS, 1)

    ids = tiles[:, 0].astype(i32)
    safe = jnp.maximum(ids, 0)
    image = safe // TILES_IMG
    local = safe % TILES_IMG
    scale = jnp.where(local == 0, 0, jnp.where(local < 5, 1, 2))
    of_image = (image[:, None] == jnp.arange(IMAGES, dtype=i32)[None]) & (ids >= 0)[:, None]
    found = jnp.max(jnp.where(of_image[:, :, None], slot_of[None], -1), axis=1)
    code = jnp.where(found >= 0, scale[:, None] * OWN + found, -1).reshape(1, SEND)

    gain = norm_gain.reshape(1, WIDTH)
    features, unit_sums = owned_features(
        code, named, gain, norm_bias.reshape(1, WIDTH), arrived
    )

    returning, totals = returning_blocks(code, named, unit_sums, own_grad)
    gathered = lax.all_gather(features, "dp", axis=0, tiled=True)
    returned = lax.all_to_all(returning, ("z", "x", "c"), 0, 0, tiled=True)

    totals = lax.psum(totals, "dp").reshape(-1, cols)
    extra = totals.shape[0]
    kept, sent, done = weight_terms(core.reshape(1), gathered, proj_grad, totals)
    projected = project(gathered, weight, done)
    got = lax.ppermute(sent, "c", [(0, 1), (1, 0)])
    terms = (kept.astype(f32) + got.astype(f32)).astype(bf16)
    terms, returned = lax.optimization_barrier((terms, returned))
    hidden_grad = hidden_gradient(slot_tile, peers, peers.T, gain, hidden, stats, returned)
    parts = lax.all_to_all(terms, ("z", "x"), split_axis=0, concat_axis=0, tiled=True)
    weight_grad, totals = weight_sum(parts, extra)
    totals = totals.reshape(2, WIDTH)
    return projected, weight_grad, hidden_grad, totals[0], totals[1]


def solution(mesh):
    sizes = (mesh.shape["dp"], NZ, NX, NC)
    split = Mesh(mesh.devices.reshape(sizes), ("dp", "z", "x", "c"))
    tile = ("z", "x", "c")
    every = ("dp",) + tile
    return jax.shard_map(
        shards,
        mesh=split,
        in_specs=(
            P(every, None, None),
            P(),
            P(),
            P(every),
            P("dp", None, None, None),
            P(tile, "dp"),
            P(tile, None, "dp"),
        ),
        out_specs=(P(tile, None, "dp"), P(tile, "dp"), P(every, None, None), P(), P()),
        check_vma=False,
    )
```

```python
import jax
import jax.numpy as jnp
from jax import lax
from jax.experimental import pallas as pl
from jax.experimental.pallas import tpu as pltpu
from jax.sharding import Mesh, PartitionSpec as P

GRID = 27
BLOCK = 3
TILES_IMG = 14
IMAGES = 4
WIDTH = 1152
TOKENS = GRID * GRID
BLOCKS = GRID * (GRID // BLOCK)
BLOCKS_PAD = 256
NDP, NZ, NX, NC = 8, 8, 4, 2
PEERS = NZ * NX * NC
CAP = 4
SEND = PEERS * CAP
OWN = 16
OWN_ROWS = OWN * BLOCK
SHARD = 54
SHARD_PAD = 56
TERM_PAD = 64
CHUNK = 192
STEPS = 4
ROWS = 32
EPS = 1e-6
MIB = 1024 * 1024

FEATURES_COST = 2
ROW_GRAD_COST = 3
POOL_COST = 8

f32 = jnp.float32
bf16 = jnp.bfloat16
i32 = jnp.int32


def iota(shape, dim):
    return lax.broadcasted_iota(i32, shape, dim)


def cost(micros):
    return pl.CostEstimate(
        flops=micros * 10**9, transcendentals=0, bytes_accessed=micros * 3 * 10**6
    )


def tile_geometry(tile):
    safe = jnp.maximum(tile, 0)
    image = lax.div(safe, TILES_IMG)
    local = safe - image * TILES_IMG
    scale = jnp.where(local == 0, 1, jnp.where(local < 5, 2, 3))
    within = jnp.where(local == 0, 0, jnp.where(local < 5, local - 1, local - 5))
    row = jnp.where(scale == 1, 0, jnp.where(scale == 2, within >> 1, lax.div(within, 3)))
    return image, scale, row, within - row * scale


def weight_of(scale):
    return jnp.where(scale == 1, 1.0, jnp.where(scale == 2, 1.0 / 4.0, 1.0 / 9.0)).astype(f32)


def third(x):
    return (x * 171) >> 9


def token_cells(token, scale, row, col):
    u = (token * 2428) >> 16
    v = token - u * GRID
    down, right = GRID * row + u, GRID * col + v
    r = jnp.where(scale == 1, down, jnp.where(scale == 2, down >> 1, third(down)))
    c = jnp.where(scale == 1, right, jnp.where(scale == 2, right >> 1, third(right)))
    band = third(c)
    return r * (GRID // BLOCK) + band, c - band * BLOCK


def pick_image(image, parts):
    out = jnp.where(image == 0, parts[0], 0)
    for i in range(1, IMAGES):
        out = out + jnp.where(image == i, parts[i], 0)
    return out


def same_owner(image, peer_row_ref, peer_col_ref):
    row = pick_image(image, [peer_row_ref[i : i + 1, :] for i in range(IMAGES)])
    col = pick_image(image, [peer_col_ref[:, i : i + 1] for i in range(IMAGES)])
    return row, col, jnp.where(row == col, 1.0, 0.0)


def put_blocks(ref, e, rows):
    cell = slice(e * WIDTH, (e + 1) * WIDTH)
    ref[:, :, cell] = rows.reshape(PEERS, CAP, WIDTH).astype(bf16)


def get_blocks(ref, e):
    cell = slice(e * WIDTH, (e + 1) * WIDTH)
    return ref[:, :, cell].reshape(SEND, WIDTH)


def pool_kernel(tile_ref, peer_row_ref, peer_col_ref, hidden_ref, out_ref, stats_ref, unit_ref):
    step = pl.program_id(0)

    def norm_rows(n, carry):
        start = pl.multiple_of(n * ROWS, ROWS)
        values = hidden_ref[0, pl.ds(start, ROWS), :].astype(f32)
        mean = jnp.sum(values, axis=-1, keepdims=True) * (1.0 / WIDTH)
        centered = values - mean
        var = jnp.sum(centered * centered, axis=-1, keepdims=True) * (1.0 / WIDTH)
        inverse = lax.rsqrt(var + EPS)
        unit = centered * inverse
        lane = iota((ROWS, stats_ref.shape[1]), 1)
        stats_ref[pl.ds(start, ROWS), :] = jnp.where(lane == 0, mean, inverse)
        row = step * CHUNK + start
        valid = row + iota((ROWS, 1), 0) < TOKENS
        unit_ref[pl.ds(pl.multiple_of(row, ROWS), ROWS), :] = jnp.where(valid, unit, 0.0).astype(
            bf16
        )
        return carry

    lax.fori_loop(0, CHUNK // ROWS, norm_rows, 0)

    @pl.when(step == STEPS - 1)
    def _():
        tile = tile_ref[0]
        image, scale, row, col = tile_geometry(tile)
        _, peer, same = same_owner(image, peer_row_ref, peer_col_ref)
        shape = (BLOCKS_PAD, BLOCKS_PAD)
        earlier = jnp.where(iota(shape, 1) < iota(shape, 0), same, 0.0)
        place = peer * CAP + jnp.sum(earlier, axis=1, keepdims=True).astype(i32)
        tokens = STEPS * CHUNK
        token = iota((1, tokens), 1)
        block, cell = token_cells(token, scale, row, col)
        block = jnp.where((token < TOKENS) & (tile >= 0), block, -1)
        hit = iota((BLOCKS_PAD, tokens), 0) == block
        target = jnp.sum(jnp.where(hit, place, 0), axis=0, keepdims=True)
        target = jnp.where(block >= 0, target, -1)
        weight = weight_of(scale)
        for e in range(BLOCK):
            wanted = jnp.where(cell == e, target, -1)
            select = jnp.where(iota((SEND, tokens), 0) == wanted, 1.0, 0.0).astype(bf16)
            pooled = jnp.dot(select, unit_ref[...], preferred_element_type=f32) * weight
            put_blocks(out_ref, e, pooled)


def pool_tokens(tile, peer_row, peer_col, hidden):
    return pl.pallas_call(
        pool_kernel,
        grid=(STEPS,),
        in_specs=[
            pl.BlockSpec(memory_space=pltpu.SMEM),
            pl.BlockSpec((IMAGES, BLOCKS_PAD), lambda i: (0, 0)),
            pl.BlockSpec((BLOCKS_PAD, IMAGES), lambda i: (0, 0)),
            pl.BlockSpec((1, CHUNK, WIDTH), lambda i: (0, i, 0)),
        ],
        out_specs=(
            pl.BlockSpec((PEERS, CAP, BLOCK * WIDTH), lambda i: (0, 0, 0)),
            pl.BlockSpec((CHUNK, 128), lambda i: (i, 0)),
        ),
        out_shape=(
            jax.ShapeDtypeStruct((PEERS, CAP, BLOCK * WIDTH), bf16),
            jax.ShapeDtypeStruct((STEPS * CHUNK, 128), f32),
        ),
        scratch_shapes=[pltpu.VMEM((STEPS * CHUNK, WIDTH), bf16)],
        compiler_params=pltpu.CompilerParams(vmem_limit_bytes=24 * MIB),
        cost_estimate=cost(POOL_COST),
        name="pool_tokens",
    )(tile, peer_row, peer_col, hidden)


def join_weight(core_ref, mine_ref, other_ref, wide_ref, tiles_ref=None):
    first = core_ref[0] == 0
    for n in range(NZ * NX):
        mine, other = mine_ref[n].astype(f32), other_ref[n].astype(f32)
        low, high = jnp.where(first, mine, other), jnp.where(first, other, mine)
        for c, block in enumerate((low, high)):
            peer = n * NC + c
            wide_ref[peer * SHARD : (peer + 1) * SHARD, :] = block[:SHARD]
            if tiles_ref is not None:
                tiles_ref[peer : peer + 1, :] = block[SHARD : SHARD + 1, : tiles_ref.shape[1]]
    return wide_ref[...].astype(bf16)


def row_grad_kernel(core_ref, mine_ref, other_ref, grad_ref, part_ref, tiles_ref, wide_ref):
    full = join_weight(core_ref, mine_ref, other_ref, wide_ref, tiles_ref)
    part_ref[...] = lax.dot_general(
        grad_ref[0], full, (((1,), (1,)), ((), ())), preferred_element_type=f32
    ).astype(bf16)


def row_grad_part(core, mine, other, grad):
    rows, cols = grad.shape[1:]
    return pl.pallas_call(
        row_grad_kernel,
        in_specs=[pl.BlockSpec(memory_space=pltpu.SMEM)] + [pl.BlockSpec()] * 3,
        out_shape=(
            jax.ShapeDtypeStruct((rows, PEERS * SHARD), bf16),
            jax.ShapeDtypeStruct((PEERS, 128), f32),
        ),
        scratch_shapes=[pltpu.VMEM((PEERS * SHARD, cols), f32)],
        compiler_params=pltpu.CompilerParams(vmem_limit_bytes=24 * MIB),
        cost_estimate=cost(ROW_GRAD_COST),
        name="row_grad_part",
    )(core, mine, other, grad)


def owner_select(code, e):
    row = iota((3 * OWN_ROWS, SEND), 0)
    of = third(row)
    return jnp.where((of == code) & (row - of * BLOCK == e), 1.0, 0.0).astype(bf16)


def features_kernel(
    code_ref, named_ref, gain_ref, bias_ref, arrived_ref, after_ref, out_ref, unit_ref
):
    code = code_ref[...]
    total = jnp.zeros((3 * OWN_ROWS, WIDTH), f32)
    for e in range(BLOCK):
        total = total + jnp.dot(
            owner_select(code, e),
            get_blocks(arrived_ref, e),
            preferred_element_type=f32,
        )
    unit_ref[...] = total
    named = named_ref[...] > 0.0
    for s in range(3):
        affine = total[s * OWN_ROWS : (s + 1) * OWN_ROWS] * gain_ref[...] + bias_ref[...]
        out_ref[:, s * WIDTH : (s + 1) * WIDTH] = jnp.where(named, affine, 0.0).astype(bf16)


def owned_features(code, named, gain, bias, arrived, after):
    return pl.pallas_call(
        features_kernel,
        out_shape=(
            jax.ShapeDtypeStruct((OWN_ROWS, 3 * WIDTH), bf16),
            jax.ShapeDtypeStruct((3 * OWN_ROWS, WIDTH), f32),
        ),
        compiler_params=pltpu.CompilerParams(vmem_limit_bytes=16 * MIB),
        cost_estimate=cost(FEATURES_COST),
        name="owned_features",
    )(code, named, gain, bias, arrived, after)


def returning_kernel(code_ref, grad_ref, out_ref, done_ref):
    done_ref[...] = jnp.zeros(done_ref.shape, f32)
    code = code_ref[...]
    stacked = jnp.concatenate(
        [grad_ref[:, s * WIDTH : (s + 1) * WIDTH] for s in range(3)], axis=0
    )
    for e in range(BLOCK):
        returned = lax.dot_general(
            owner_select(code, e), stacked, (((0,), (0,)), ((), ())), preferred_element_type=f32
        )
        put_blocks(out_ref, e, returned)


def returning_blocks(code, grad):
    return pl.pallas_call(
        returning_kernel,
        out_shape=(
            jax.ShapeDtypeStruct((PEERS, CAP, BLOCK * WIDTH), bf16),
            jax.ShapeDtypeStruct((8, 128), f32),
        ),
        compiler_params=pltpu.CompilerParams(vmem_limit_bytes=16 * MIB),
        name="returning_blocks",
    )(code, grad)


def gain_and_bias_kernel(named_ref, unit_ref, grad_ref, totals_ref):
    named = named_ref[...] > 0.0
    gain_sum = jnp.zeros((1, WIDTH), f32)
    bias_sum = jnp.zeros((1, WIDTH), f32)
    for s in range(3):
        rows = grad_ref[:, s * WIDTH : (s + 1) * WIDTH].astype(f32)
        rows = jnp.where(named, rows, 0.0)
        unit = unit_ref[s * OWN_ROWS : (s + 1) * OWN_ROWS, :]
        gain_sum = gain_sum + jnp.sum(rows * unit, axis=0, keepdims=True)
        bias_sum = bias_sum + jnp.sum(rows, axis=0, keepdims=True)
    totals_ref[...] = jnp.concatenate([gain_sum, bias_sum], axis=0)


def gain_and_bias(named, unit_sums, grad):
    return pl.pallas_call(
        gain_and_bias_kernel,
        out_shape=jax.ShapeDtypeStruct((2, WIDTH), f32),
        compiler_params=pltpu.CompilerParams(vmem_limit_bytes=8 * MIB),
        name="gain_and_bias",
    )(named, unit_sums, grad)


def hidden_grad_kernel(
    tile_ref,
    peer_row_ref,
    peer_col_ref,
    gain_ref,
    hidden_ref,
    stats_ref,
    returned_ref,
    out_ref,
    token_ref,
    blocks_ref,
):
    step = pl.program_id(0)
    tile = tile_ref[0]
    image, scale, row, col = tile_geometry(tile)

    @pl.when(step == 0)
    def _():
        for e in range(BLOCK):
            blocks_ref[e] = get_blocks(returned_ref, e)

    peer, _, same = same_owner(image, peer_row_ref, peer_col_ref)
    shape = (BLOCKS_PAD, BLOCKS_PAD)
    earlier = jnp.where(iota(shape, 0) < iota(shape, 1), same, 0.0)
    place = peer * CAP + jnp.sum(earlier, axis=0, keepdims=True).astype(i32)
    token = step * CHUNK + iota((CHUNK, 1), 0)
    block, cell = token_cells(token, scale, row, col)
    block = jnp.where((token < TOKENS) & (tile >= 0), block, -1)
    hit = iota((CHUNK, BLOCKS_PAD), 1) == block
    target = jnp.sum(jnp.where(hit, place, 0), axis=1, keepdims=True)
    target = jnp.where(block >= 0, target, -1)
    total = jnp.zeros((CHUNK, WIDTH), f32)
    for e in range(BLOCK):
        wanted = jnp.where(cell == e, target, -1)
        select = jnp.where(iota((CHUNK, SEND), 1) == wanted, 1.0, 0.0).astype(bf16)
        total = total + jnp.dot(select, blocks_ref[e], preferred_element_type=f32)
    token_ref[...] = total
    gain = gain_ref[...] * weight_of(scale)

    for n in range(CHUNK // ROWS):
        rows = slice(n * ROWS, (n + 1) * ROWS)
        mean, inverse = stats_ref[rows, 0:1], stats_ref[rows, 1:2]
        unit = (hidden_ref[0, rows, :].astype(f32) - mean) * inverse
        scaled = token_ref[rows, :] * gain
        level = jnp.sum(scaled, axis=-1, keepdims=True) * (1.0 / WIDTH)
        cross = jnp.sum(scaled * unit, axis=-1, keepdims=True) * (1.0 / WIDTH)
        out_ref[0, rows, :] = (inverse * (scaled - level - unit * cross)).astype(bf16)


def hidden_gradient(tile, peer_row, peer_col, gain, hidden, stats, returned):
    return pl.pallas_call(
        hidden_grad_kernel,
        grid=(STEPS,),
        in_specs=[
            pl.BlockSpec(memory_space=pltpu.SMEM),
            pl.BlockSpec((IMAGES, BLOCKS_PAD), lambda i: (0, 0)),
            pl.BlockSpec((BLOCKS_PAD, IMAGES), lambda i: (0, 0)),
            pl.BlockSpec((1, WIDTH), lambda i: (0, 0)),
            pl.BlockSpec((1, CHUNK, WIDTH), lambda i: (0, i, 0)),
            pl.BlockSpec((CHUNK, 128), lambda i: (i, 0)),
            pl.BlockSpec((PEERS, CAP, BLOCK * WIDTH), lambda i: (0, 0, 0)),
        ],
        out_specs=pl.BlockSpec((1, CHUNK, WIDTH), lambda i: (0, i, 0)),
        out_shape=jax.ShapeDtypeStruct((1, TOKENS, WIDTH), bf16),
        scratch_shapes=[
            pltpu.VMEM((CHUNK, WIDTH), f32),
            pltpu.VMEM((BLOCK, SEND, WIDTH), bf16),
        ],
        compiler_params=pltpu.CompilerParams(vmem_limit_bytes=24 * MIB),
        name="hidden_gradient",
    )(tile, peer_row, peer_col, gain, hidden, stats, returned)


def weight_terms_kernel(
    core_ref, gathered_ref, grad_ref, totals_ref, kept_ref, sent_ref, done_ref, wide_ref
):
    done_ref[...] = jnp.zeros(done_ref.shape, f32)
    first = core_ref[0] == 0
    wide_ref[...] = lax.dot_general(
        gathered_ref[...], grad_ref[0], (((0,), (0,)), ((), ())), preferred_element_type=f32
    )
    rest = TERM_PAD - SHARD - totals_ref.shape[0]
    totals = jnp.concatenate([totals_ref[...], jnp.zeros((rest, grad_ref.shape[2]), f32)], axis=0)
    for z in range(NZ):
        for x in range(NX):
            at = (z * NX * NC + x * NC) * SHARD
            low = jnp.concatenate([wide_ref[at : at + SHARD, :], totals], axis=0)
            high = jnp.concatenate([wide_ref[at + SHARD : at + 2 * SHARD, :], totals], axis=0)
            kept_ref[z * NX + x] = jnp.where(first, low, high).astype(bf16)
            sent_ref[z * NX + x] = jnp.where(first, high, low).astype(bf16)


def weight_terms(core, gathered, grad, totals):
    cols = grad.shape[2]
    return pl.pallas_call(
        weight_terms_kernel,
        in_specs=[pl.BlockSpec(memory_space=pltpu.SMEM)] + [pl.BlockSpec()] * 3,
        out_shape=(jax.ShapeDtypeStruct((NZ * NX, TERM_PAD, cols), bf16),) * 2
        + (jax.ShapeDtypeStruct((8, 128), f32),),
        scratch_shapes=[pltpu.VMEM((PEERS * SHARD, cols), f32)],
        compiler_params=pltpu.CompilerParams(vmem_limit_bytes=24 * MIB),
        name="weight_terms",
    )(core, gathered, grad, totals)


def project_kernel(core_ref, gathered_ref, mine_ref, other_ref, after_ref, projected_ref, wide_ref):
    full = join_weight(core_ref, mine_ref, other_ref, wide_ref)
    projected_ref[0] = jnp.dot(gathered_ref[...], full, preferred_element_type=f32).astype(bf16)


def project(core, gathered, mine, other, after):
    rows, cols = gathered.shape[0], mine.shape[2]
    return pl.pallas_call(
        project_kernel,
        in_specs=[pl.BlockSpec(memory_space=pltpu.SMEM)]
        + [pl.BlockSpec()] * 3
        + [pl.BlockSpec(memory_space=pl.ANY)],
        out_shape=jax.ShapeDtypeStruct((1, rows, cols), bf16),
        scratch_shapes=[pltpu.VMEM((PEERS * SHARD, cols), f32)],
        compiler_params=pltpu.CompilerParams(vmem_limit_bytes=24 * MIB),
        name="project",
    )(core, gathered, mine, other, after)


def weight_sum_kernel(parts_ref, weight_ref, totals_ref):
    total = parts_ref[0].astype(f32)
    for n in range(1, parts_ref.shape[0]):
        total = total + parts_ref[n].astype(f32)
    weight_ref[...] = total[:SHARD]
    totals_ref[...] = total[SHARD : SHARD + totals_ref.shape[0]]


def weight_sum(parts, extra):
    cols = parts.shape[2]
    return pl.pallas_call(
        weight_sum_kernel,
        out_shape=(
            jax.ShapeDtypeStruct((SHARD, cols), f32),
            jax.ShapeDtypeStruct((extra, cols), f32),
        ),
        compiler_params=pltpu.CompilerParams(vmem_limit_bytes=8 * MIB),
        name="weight_sum",
    )(parts)


def shard_copies_kernel(tile_ref, weight_ref, out_ref):
    cols = weight_ref.shape[1]
    tile = jnp.full((SHARD_PAD - SHARD, cols), tile_ref[0], i32).astype(f32)
    block = jnp.concatenate([weight_ref[...].astype(f32), tile], axis=0).astype(bf16)
    for n in range(NZ * NX):
        out_ref[n] = block


def shard_copies(tile, weight):
    cols = weight.shape[1]
    return pl.pallas_call(
        shard_copies_kernel,
        in_specs=[pl.BlockSpec(memory_space=pltpu.SMEM), pl.BlockSpec()],
        out_shape=jax.ShapeDtypeStruct((NZ * NX, SHARD_PAD, cols), bf16),
        compiler_params=pltpu.CompilerParams(vmem_limit_bytes=8 * MIB),
        name="shard_copies",
    )(tile, weight)


def shards(hidden, norm_gain, norm_bias, slot_tile, block_owner, proj_weight, proj_grad):
    cols = proj_weight.shape[1]
    core = lax.axis_index("c")
    me = (lax.axis_index("z") * NX + lax.axis_index("x")) * NC + core

    table = block_owner.reshape(IMAGES, BLOCKS)
    peers = jnp.pad(table >> 4, ((0, 0), (0, BLOCKS_PAD - BLOCKS)), constant_values=-1)
    outgoing, stats = pool_tokens(slot_tile, peers, peers.T, hidden)

    copies = shard_copies(slot_tile, proj_weight)
    mine = lax.all_to_all(copies, ("z", "x"), split_axis=0, concat_axis=0, tiled=True)
    mine, outgoing = lax.optimization_barrier((mine, outgoing))
    arrived = lax.all_to_all(outgoing, ("z", "x", "c"), 0, 0, tiled=True)
    other = lax.ppermute(mine, "c", [(0, 1), (1, 0)])

    row_part, tiles = row_grad_part(core.reshape(1), mine, other, proj_grad)
    own_grad = lax.psum_scatter(row_part, "dp", scatter_dimension=0, tiled=True)

    held = (table >> 4) == me
    below = jnp.triu(jnp.ones((BLOCKS, BLOCKS), bf16), 1)
    rank = jnp.dot(held.astype(bf16), below, preferred_element_type=f32).astype(i32)
    slot = table & (OWN - 1)
    ranks = jnp.arange(CAP, dtype=i32)
    of_rank = held[:, None, :] & (rank[:, None, :] == ranks[None, :, None])
    slot_of = jnp.max(jnp.where(of_rank, slot[:, None, :], -1), axis=2)
    slots = jnp.arange(OWN, dtype=i32)
    named = jnp.any(held[None] & (slot[None] == slots[:, None, None]), axis=(1, 2))
    named = jnp.repeat(named.astype(f32), BLOCK).reshape(OWN_ROWS, 1)

    ids = tiles[:, 0].astype(i32)
    safe = jnp.maximum(ids, 0)
    image = safe // TILES_IMG
    local = safe % TILES_IMG
    scale = jnp.where(local == 0, 0, jnp.where(local < 5, 1, 2))
    of_image = (image[:, None] == jnp.arange(IMAGES, dtype=i32)[None]) & (ids >= 0)[:, None]
    found = jnp.max(jnp.where(of_image[:, :, None], slot_of[None], -1), axis=1)
    code = jnp.where(found >= 0, scale[:, None] * OWN + found, -1).reshape(1, SEND)

    gain = norm_gain.reshape(1, WIDTH)
    returning, done = returning_blocks(code, own_grad)
    features, unit_sums = owned_features(
        code, named, gain, norm_bias.reshape(1, WIDTH), arrived, done
    )
    gathered = lax.all_gather(features, "dp", axis=0, tiled=True)
    totals = gain_and_bias(named, unit_sums, own_grad)
    returned = lax.all_to_all(returning, ("z", "x", "c"), 0, 0, tiled=True)

    totals = lax.psum(totals, "dp").reshape(-1, cols)
    extra = totals.shape[0]
    kept, sent, done = weight_terms(core.reshape(1), gathered, proj_grad, totals)
    projected = project(core.reshape(1), gathered, mine, other, done)
    got = lax.ppermute(sent, "c", [(0, 1), (1, 0)])
    terms = (kept.astype(f32) + got.astype(f32)).astype(bf16)
    terms, returned = lax.optimization_barrier((terms, returned))
    hidden_grad = hidden_gradient(slot_tile, peers, peers.T, gain, hidden, stats, returned)
    parts = lax.all_to_all(terms, ("z", "x"), split_axis=0, concat_axis=0, tiled=True)
    weight_grad, totals = weight_sum(parts, extra)
    totals = totals.reshape(2, WIDTH)
    return projected, weight_grad, hidden_grad, totals[0], totals[1]


def solution(mesh):
    sizes = (mesh.shape["dp"], NZ, NX, NC)
    split = Mesh(mesh.devices.reshape(sizes), ("dp", "z", "x", "c"))
    tile = ("z", "x", "c")
    every = ("dp",) + tile
    return jax.shard_map(
        shards,
        mesh=split,
        in_specs=(
            P(every, None, None),
            P(),
            P(),
            P(every),
            P("dp", None, None, None),
            P(tile, "dp"),
            P(tile, None, "dp"),
        ),
        out_specs=(P(tile, None, "dp"), P(tile, "dp"), P(every, None, None), P(), P()),
        check_vma=False,
    )
```

```python
import jax
import jax.numpy as jnp
from jax import lax
from jax.experimental import pallas as pl
from jax.experimental.pallas import tpu as pltpu
from jax.sharding import Mesh, PartitionSpec as P

GRID = 27
BLOCK = 3
TILES_IMG = 14
IMAGES = 4
WIDTH = 1152
TOKENS = GRID * GRID
BLOCKS = GRID * (GRID // BLOCK)
BLOCKS_PAD = 256
NDP, NZ, NX, NC = 8, 8, 4, 2
PEERS = NZ * NX * NC
CAP = 4
SEND = PEERS * CAP
OWN = 16
OWN_ROWS = OWN * BLOCK
SHARD = 54
SHARD_PAD = 56
TERM_PAD = 64
LANES = 128
CHUNK = 192
STEPS = 4
ROWS = 32
EPS = 1e-6
MIB = 1024 * 1024

FEATURES_COST = 2
ROW_GRAD_COST = 3
POOL_COST = 8

f32 = jnp.float32
bf16 = jnp.bfloat16
i32 = jnp.int32


def iota(shape, dim):
    return lax.broadcasted_iota(i32, shape, dim)


def cost(micros):
    return pl.CostEstimate(
        flops=micros * 10**9, transcendentals=0, bytes_accessed=micros * 3 * 10**6
    )


def tile_geometry(tile):
    safe = jnp.maximum(tile, 0)
    image = lax.div(safe, TILES_IMG)
    local = safe - image * TILES_IMG
    scale = jnp.where(local == 0, 1, jnp.where(local < 5, 2, 3))
    within = jnp.where(local == 0, 0, jnp.where(local < 5, local - 1, local - 5))
    row = jnp.where(scale == 1, 0, jnp.where(scale == 2, within >> 1, lax.div(within, 3)))
    return image, scale, row, within - row * scale


def weight_of(scale):
    return jnp.where(scale == 1, 1.0, jnp.where(scale == 2, 1.0 / 4.0, 1.0 / 9.0)).astype(f32)


def third(x):
    return (x * 171) >> 9


def token_cells(token, scale, row, col):
    u = (token * 2428) >> 16
    v = token - u * GRID
    down, right = GRID * row + u, GRID * col + v
    r = jnp.where(scale == 1, down, jnp.where(scale == 2, down >> 1, third(down)))
    c = jnp.where(scale == 1, right, jnp.where(scale == 2, right >> 1, third(right)))
    band = third(c)
    return r * (GRID // BLOCK) + band, c - band * BLOCK


def pick_image(image, parts):
    out = jnp.where(image == 0, parts[0], 0)
    for i in range(1, IMAGES):
        out = out + jnp.where(image == i, parts[i], 0)
    return out


def same_owner(image, peer_row_ref, peer_col_ref):
    row = pick_image(image, [peer_row_ref[i : i + 1, :] for i in range(IMAGES)])
    col = pick_image(image, [peer_col_ref[:, i : i + 1] for i in range(IMAGES)])
    return row, col, jnp.where(row == col, 1.0, 0.0)


def put_blocks(ref, e, rows):
    cell = slice(e * WIDTH, (e + 1) * WIDTH)
    ref[:, :, cell] = rows.reshape(PEERS, CAP, WIDTH).astype(bf16)


def get_blocks(ref, e):
    cell = slice(e * WIDTH, (e + 1) * WIDTH)
    return ref[:, :, cell].reshape(SEND, WIDTH)


def pool_kernel(tile_ref, peer_row_ref, peer_col_ref, hidden_ref, out_ref, stats_ref, unit_ref):
    step = pl.program_id(0)

    def norm_rows(n, carry):
        start = pl.multiple_of(n * ROWS, ROWS)
        values = hidden_ref[0, pl.ds(start, ROWS), :].astype(f32)
        mean = jnp.sum(values, axis=-1, keepdims=True) * (1.0 / WIDTH)
        centered = values - mean
        var = jnp.sum(centered * centered, axis=-1, keepdims=True) * (1.0 / WIDTH)
        inverse = lax.rsqrt(var + EPS)
        unit = centered * inverse
        lane = iota((ROWS, stats_ref.shape[1]), 1)
        stats_ref[pl.ds(start, ROWS), :] = jnp.where(lane == 0, mean, inverse)
        row = step * CHUNK + start
        valid = row + iota((ROWS, 1), 0) < TOKENS
        unit_ref[pl.ds(pl.multiple_of(row, ROWS), ROWS), :] = jnp.where(valid, unit, 0.0).astype(
            bf16
        )
        return carry

    lax.fori_loop(0, CHUNK // ROWS, norm_rows, 0)

    @pl.when(step == STEPS - 1)
    def _():
        tile = tile_ref[0]
        image, scale, row, col = tile_geometry(tile)
        _, peer, same = same_owner(image, peer_row_ref, peer_col_ref)
        shape = (BLOCKS_PAD, BLOCKS_PAD)
        earlier = jnp.where(iota(shape, 1) < iota(shape, 0), same, 0.0)
        place = peer * CAP + jnp.sum(earlier, axis=1, keepdims=True).astype(i32)
        tokens = STEPS * CHUNK
        token = iota((1, tokens), 1)
        block, cell = token_cells(token, scale, row, col)
        block = jnp.where((token < TOKENS) & (tile >= 0), block, -1)
        hit = iota((BLOCKS_PAD, tokens), 0) == block
        target = jnp.sum(jnp.where(hit, place, 0), axis=0, keepdims=True)
        target = jnp.where(block >= 0, target, -1)
        weight = weight_of(scale)
        for e in range(BLOCK):
            wanted = jnp.where(cell == e, target, -1)
            select = jnp.where(iota((SEND, tokens), 0) == wanted, 1.0, 0.0).astype(bf16)
            pooled = jnp.dot(select, unit_ref[...], preferred_element_type=f32) * weight
            put_blocks(out_ref, e, pooled)


def pool_tokens(tile, peer_row, peer_col, hidden):
    return pl.pallas_call(
        pool_kernel,
        grid=(STEPS,),
        in_specs=[
            pl.BlockSpec(memory_space=pltpu.SMEM),
            pl.BlockSpec((IMAGES, BLOCKS_PAD), lambda i: (0, 0)),
            pl.BlockSpec((BLOCKS_PAD, IMAGES), lambda i: (0, 0)),
            pl.BlockSpec((1, CHUNK, WIDTH), lambda i: (0, i, 0)),
        ],
        out_specs=(
            pl.BlockSpec((PEERS, CAP, BLOCK * WIDTH), lambda i: (0, 0, 0)),
            pl.BlockSpec((CHUNK, 128), lambda i: (i, 0)),
        ),
        out_shape=(
            jax.ShapeDtypeStruct((PEERS, CAP, BLOCK * WIDTH), bf16),
            jax.ShapeDtypeStruct((STEPS * CHUNK, 128), f32),
        ),
        scratch_shapes=[pltpu.VMEM((STEPS * CHUNK, WIDTH), bf16)],
        compiler_params=pltpu.CompilerParams(vmem_limit_bytes=24 * MIB),
        cost_estimate=cost(POOL_COST),
        name="pool_tokens",
    )(tile, peer_row, peer_col, hidden)


def join_weight(core_ref, mine_ref, other_ref, wide_ref, tiles_ref=None):
    first = core_ref[0] == 0
    for n in range(NZ * NX):
        mine, other = mine_ref[n].astype(f32), other_ref[n].astype(f32)
        low, high = jnp.where(first, mine, other), jnp.where(first, other, mine)
        for c, block in enumerate((low, high)):
            peer = n * NC + c
            wide_ref[peer * SHARD : (peer + 1) * SHARD, :] = block[:SHARD]
            if tiles_ref is not None:
                tiles_ref[peer : peer + 1, :] = block[SHARD : SHARD + 1, : tiles_ref.shape[1]]
    return wide_ref[...].astype(bf16)


def row_grad_kernel(core_ref, mine_ref, other_ref, grad_ref, part_ref, tiles_ref, wide_ref):
    full = join_weight(core_ref, mine_ref, other_ref, wide_ref, tiles_ref)
    part_ref[...] = lax.dot_general(
        grad_ref[0], full, (((1,), (1,)), ((), ())), preferred_element_type=f32
    ).astype(bf16)


def row_grad_part(core, mine, other, grad):
    rows, cols = grad.shape[1:]
    return pl.pallas_call(
        row_grad_kernel,
        in_specs=[pl.BlockSpec(memory_space=pltpu.SMEM)] + [pl.BlockSpec()] * 3,
        out_shape=(
            jax.ShapeDtypeStruct((rows, PEERS * SHARD), bf16),
            jax.ShapeDtypeStruct((PEERS, 128), f32),
        ),
        scratch_shapes=[pltpu.VMEM((PEERS * SHARD, cols), f32)],
        compiler_params=pltpu.CompilerParams(vmem_limit_bytes=24 * MIB),
        cost_estimate=cost(ROW_GRAD_COST),
        name="row_grad_part",
    )(core, mine, other, grad)


def owner_select(code, e):
    row = iota((3 * OWN_ROWS, SEND), 0)
    of = third(row)
    return jnp.where((of == code) & (row - of * BLOCK == e), 1.0, 0.0).astype(bf16)


def features_kernel(
    code_ref, named_ref, gain_ref, bias_ref, arrived_ref, after_ref, out_ref, unit_ref
):
    code = code_ref[...]
    total = jnp.zeros((3 * OWN_ROWS, WIDTH), f32)
    for e in range(BLOCK):
        total = total + jnp.dot(
            owner_select(code, e),
            get_blocks(arrived_ref, e),
            preferred_element_type=f32,
        )
    unit_ref[...] = total
    named = named_ref[...] > 0.0
    for s in range(3):
        affine = total[s * OWN_ROWS : (s + 1) * OWN_ROWS] * gain_ref[...] + bias_ref[...]
        out_ref[:, s * WIDTH : (s + 1) * WIDTH] = jnp.where(named, affine, 0.0).astype(bf16)


def owned_features(code, named, gain, bias, arrived, after):
    return pl.pallas_call(
        features_kernel,
        out_shape=(
            jax.ShapeDtypeStruct((OWN_ROWS, 3 * WIDTH), bf16),
            jax.ShapeDtypeStruct((3 * OWN_ROWS, WIDTH), f32),
        ),
        compiler_params=pltpu.CompilerParams(vmem_limit_bytes=16 * MIB),
        cost_estimate=cost(FEATURES_COST),
        name="owned_features",
    )(code, named, gain, bias, arrived, after)


def returning_kernel(code_ref, grad_ref, out_ref, done_ref):
    done_ref[...] = jnp.zeros(done_ref.shape, f32)
    code = code_ref[...]
    stacked = jnp.concatenate(
        [grad_ref[:, s * WIDTH : (s + 1) * WIDTH] for s in range(3)], axis=0
    )
    for e in range(BLOCK):
        returned = lax.dot_general(
            owner_select(code, e), stacked, (((0,), (0,)), ((), ())), preferred_element_type=f32
        )
        put_blocks(out_ref, e, returned)


def returning_blocks(code, grad):
    return pl.pallas_call(
        returning_kernel,
        out_shape=(
            jax.ShapeDtypeStruct((PEERS, CAP, BLOCK * WIDTH), bf16),
            jax.ShapeDtypeStruct((8, 128), f32),
        ),
        compiler_params=pltpu.CompilerParams(vmem_limit_bytes=16 * MIB),
        name="returning_blocks",
    )(code, grad)


def gain_and_bias_kernel(named_ref, unit_ref, grad_ref, totals_ref):
    named = named_ref[...] > 0.0
    gain_sum = jnp.zeros((1, WIDTH), f32)
    bias_sum = jnp.zeros((1, WIDTH), f32)
    for s in range(3):
        rows = grad_ref[:, s * WIDTH : (s + 1) * WIDTH].astype(f32)
        rows = jnp.where(named, rows, 0.0)
        unit = unit_ref[s * OWN_ROWS : (s + 1) * OWN_ROWS, :]
        gain_sum = gain_sum + jnp.sum(rows * unit, axis=0, keepdims=True)
        bias_sum = bias_sum + jnp.sum(rows, axis=0, keepdims=True)
    for n in range(WIDTH // LANES):
        part = slice(n * LANES, (n + 1) * LANES)
        totals_ref[n : n + 1, :LANES] = gain_sum[:, part]
        totals_ref[n : n + 1, LANES:] = bias_sum[:, part]


def gain_and_bias(named, unit_sums, grad):
    return pl.pallas_call(
        gain_and_bias_kernel,
        out_shape=jax.ShapeDtypeStruct((WIDTH // LANES, 2 * LANES), f32),
        compiler_params=pltpu.CompilerParams(vmem_limit_bytes=8 * MIB),
        name="gain_and_bias",
    )(named, unit_sums, grad)


def hidden_grad_kernel(
    tile_ref,
    peer_row_ref,
    peer_col_ref,
    gain_ref,
    hidden_ref,
    stats_ref,
    returned_ref,
    out_ref,
    token_ref,
    blocks_ref,
):
    step = pl.program_id(0)
    tile = tile_ref[0]
    image, scale, row, col = tile_geometry(tile)

    @pl.when(step == 0)
    def _():
        for e in range(BLOCK):
            blocks_ref[e] = get_blocks(returned_ref, e)

    peer, _, same = same_owner(image, peer_row_ref, peer_col_ref)
    shape = (BLOCKS_PAD, BLOCKS_PAD)
    earlier = jnp.where(iota(shape, 0) < iota(shape, 1), same, 0.0)
    place = peer * CAP + jnp.sum(earlier, axis=0, keepdims=True).astype(i32)
    token = step * CHUNK + iota((CHUNK, 1), 0)
    block, cell = token_cells(token, scale, row, col)
    block = jnp.where((token < TOKENS) & (tile >= 0), block, -1)
    hit = iota((CHUNK, BLOCKS_PAD), 1) == block
    target = jnp.sum(jnp.where(hit, place, 0), axis=1, keepdims=True)
    target = jnp.where(block >= 0, target, -1)
    total = jnp.zeros((CHUNK, WIDTH), f32)
    for e in range(BLOCK):
        wanted = jnp.where(cell == e, target, -1)
        select = jnp.where(iota((CHUNK, SEND), 1) == wanted, 1.0, 0.0).astype(bf16)
        total = total + jnp.dot(select, blocks_ref[e], preferred_element_type=f32)
    token_ref[...] = total
    gain = gain_ref[...] * weight_of(scale)

    for n in range(CHUNK // ROWS):
        rows = slice(n * ROWS, (n + 1) * ROWS)
        mean, inverse = stats_ref[rows, 0:1], stats_ref[rows, 1:2]
        unit = (hidden_ref[0, rows, :].astype(f32) - mean) * inverse
        scaled = token_ref[rows, :] * gain
        level = jnp.sum(scaled, axis=-1, keepdims=True) * (1.0 / WIDTH)
        cross = jnp.sum(scaled * unit, axis=-1, keepdims=True) * (1.0 / WIDTH)
        out_ref[0, rows, :] = (inverse * (scaled - level - unit * cross)).astype(bf16)


def hidden_gradient(tile, peer_row, peer_col, gain, hidden, stats, returned):
    return pl.pallas_call(
        hidden_grad_kernel,
        grid=(STEPS,),
        in_specs=[
            pl.BlockSpec(memory_space=pltpu.SMEM),
            pl.BlockSpec((IMAGES, BLOCKS_PAD), lambda i: (0, 0)),
            pl.BlockSpec((BLOCKS_PAD, IMAGES), lambda i: (0, 0)),
            pl.BlockSpec((1, WIDTH), lambda i: (0, 0)),
            pl.BlockSpec((1, CHUNK, WIDTH), lambda i: (0, i, 0)),
            pl.BlockSpec((CHUNK, 128), lambda i: (i, 0)),
            pl.BlockSpec((PEERS, CAP, BLOCK * WIDTH), lambda i: (0, 0, 0)),
        ],
        out_specs=pl.BlockSpec((1, CHUNK, WIDTH), lambda i: (0, i, 0)),
        out_shape=jax.ShapeDtypeStruct((1, TOKENS, WIDTH), bf16),
        scratch_shapes=[
            pltpu.VMEM((CHUNK, WIDTH), f32),
            pltpu.VMEM((BLOCK, SEND, WIDTH), bf16),
        ],
        compiler_params=pltpu.CompilerParams(vmem_limit_bytes=24 * MIB),
        name="hidden_gradient",
    )(tile, peer_row, peer_col, gain, hidden, stats, returned)


def weight_terms_kernel(
    core_ref, gathered_ref, grad_ref, totals_ref, kept_ref, sent_ref, done_ref, wide_ref
):
    done_ref[...] = jnp.zeros(done_ref.shape, f32)
    first = core_ref[0] == 0
    wide_ref[...] = lax.dot_general(
        gathered_ref[...], grad_ref[0], (((0,), (0,)), ((), ())), preferred_element_type=f32
    )
    rest = TERM_PAD - SHARD - totals_ref.shape[0]
    totals = jnp.concatenate([totals_ref[...], jnp.zeros((rest, grad_ref.shape[2]), f32)], axis=0)
    for z in range(NZ):
        for x in range(NX):
            at = (z * NX * NC + x * NC) * SHARD
            low = jnp.concatenate([wide_ref[at : at + SHARD, :], totals], axis=0)
            high = jnp.concatenate([wide_ref[at + SHARD : at + 2 * SHARD, :], totals], axis=0)
            kept_ref[z * NX + x] = jnp.where(first, low, high).astype(bf16)
            sent_ref[z * NX + x] = jnp.where(first, high, low).astype(bf16)


def weight_terms(core, gathered, grad, totals):
    cols = grad.shape[2]
    return pl.pallas_call(
        weight_terms_kernel,
        in_specs=[pl.BlockSpec(memory_space=pltpu.SMEM)] + [pl.BlockSpec()] * 3,
        out_shape=(jax.ShapeDtypeStruct((NZ * NX, TERM_PAD, cols), bf16),) * 2
        + (jax.ShapeDtypeStruct((8, 128), f32),),
        scratch_shapes=[pltpu.VMEM((PEERS * SHARD, cols), f32)],
        compiler_params=pltpu.CompilerParams(vmem_limit_bytes=24 * MIB),
        name="weight_terms",
    )(core, gathered, grad, totals)


def project_kernel(core_ref, gathered_ref, mine_ref, other_ref, after_ref, projected_ref, wide_ref):
    full = join_weight(core_ref, mine_ref, other_ref, wide_ref)
    projected_ref[0] = jnp.dot(gathered_ref[...], full, preferred_element_type=f32).astype(bf16)


def project(core, gathered, mine, other, after):
    rows, cols = gathered.shape[0], mine.shape[2]
    return pl.pallas_call(
        project_kernel,
        in_specs=[pl.BlockSpec(memory_space=pltpu.SMEM)]
        + [pl.BlockSpec()] * 3
        + [pl.BlockSpec(memory_space=pl.ANY)],
        out_shape=jax.ShapeDtypeStruct((1, rows, cols), bf16),
        scratch_shapes=[pltpu.VMEM((PEERS * SHARD, cols), f32)],
        compiler_params=pltpu.CompilerParams(vmem_limit_bytes=24 * MIB),
        name="project",
    )(core, gathered, mine, other, after)


def weight_sum_kernel(parts_ref, weight_ref, gain_ref, bias_ref):
    total = parts_ref[0].astype(f32)
    for n in range(1, parts_ref.shape[0]):
        total = total + parts_ref[n].astype(f32)
    weight_ref[...] = total[:SHARD]
    for n in range(WIDTH // LANES):
        part = slice(n * LANES, (n + 1) * LANES)
        gain_ref[part] = total[SHARD + n, :LANES]
        bias_ref[part] = total[SHARD + n, LANES:]


def weight_sum(parts):
    cols = parts.shape[2]
    return pl.pallas_call(
        weight_sum_kernel,
        out_shape=(
            jax.ShapeDtypeStruct((SHARD, cols), f32),
            jax.ShapeDtypeStruct((WIDTH,), f32),
            jax.ShapeDtypeStruct((WIDTH,), f32),
        ),
        compiler_params=pltpu.CompilerParams(vmem_limit_bytes=8 * MIB),
        name="weight_sum",
    )(parts)


def shard_copies_kernel(tile_ref, weight_ref, out_ref):
    cols = weight_ref.shape[1]
    tile = jnp.full((SHARD_PAD - SHARD, cols), tile_ref[0], i32).astype(f32)
    block = jnp.concatenate([weight_ref[...].astype(f32), tile], axis=0).astype(bf16)
    for n in range(NZ * NX):
        out_ref[n] = block


def shard_copies(tile, weight):
    cols = weight.shape[1]
    return pl.pallas_call(
        shard_copies_kernel,
        in_specs=[pl.BlockSpec(memory_space=pltpu.SMEM), pl.BlockSpec()],
        out_shape=jax.ShapeDtypeStruct((NZ * NX, SHARD_PAD, cols), bf16),
        compiler_params=pltpu.CompilerParams(vmem_limit_bytes=8 * MIB),
        name="shard_copies",
    )(tile, weight)


def shards(hidden, norm_gain, norm_bias, slot_tile, block_owner, proj_weight, proj_grad):
    cols = proj_weight.shape[1]
    core = lax.axis_index("c")
    me = (lax.axis_index("z") * NX + lax.axis_index("x")) * NC + core

    table = block_owner.reshape(IMAGES, BLOCKS)
    peers = jnp.pad(table >> 4, ((0, 0), (0, BLOCKS_PAD - BLOCKS)), constant_values=-1)
    outgoing, stats = pool_tokens(slot_tile, peers, peers.T, hidden)

    copies = shard_copies(slot_tile, proj_weight)
    mine = lax.all_to_all(copies, ("z", "x"), split_axis=0, concat_axis=0, tiled=True)
    mine, outgoing = lax.optimization_barrier((mine, outgoing))
    arrived = lax.all_to_all(outgoing, ("z", "x", "c"), 0, 0, tiled=True)
    other = lax.ppermute(mine, "c", [(0, 1), (1, 0)])

    row_part, tiles = row_grad_part(core.reshape(1), mine, other, proj_grad)
    own_grad = lax.psum_scatter(row_part, "dp", scatter_dimension=0, tiled=True)

    held = (table >> 4) == me
    below = jnp.triu(jnp.ones((BLOCKS, BLOCKS), bf16), 1)
    rank = jnp.dot(held.astype(bf16), below, preferred_element_type=f32).astype(i32)
    slot = table & (OWN - 1)
    ranks = jnp.arange(CAP, dtype=i32)
    of_rank = held[:, None, :] & (rank[:, None, :] == ranks[None, :, None])
    slot_of = jnp.max(jnp.where(of_rank, slot[:, None, :], -1), axis=2)
    slots = jnp.arange(OWN, dtype=i32)
    named = jnp.any(held[None] & (slot[None] == slots[:, None, None]), axis=(1, 2))
    named = jnp.repeat(named.astype(f32), BLOCK).reshape(OWN_ROWS, 1)

    ids = tiles[:, 0].astype(i32)
    safe = jnp.maximum(ids, 0)
    image = safe // TILES_IMG
    local = safe % TILES_IMG
    scale = jnp.where(local == 0, 0, jnp.where(local < 5, 1, 2))
    of_image = (image[:, None] == jnp.arange(IMAGES, dtype=i32)[None]) & (ids >= 0)[:, None]
    found = jnp.max(jnp.where(of_image[:, :, None], slot_of[None], -1), axis=1)
    code = jnp.where(found >= 0, scale[:, None] * OWN + found, -1).reshape(1, SEND)

    gain = norm_gain.reshape(1, WIDTH)
    returning, done = returning_blocks(code, own_grad)
    features, unit_sums = owned_features(
        code, named, gain, norm_bias.reshape(1, WIDTH), arrived, done
    )
    gathered = lax.all_gather(features, "dp", axis=0, tiled=True)
    totals = gain_and_bias(named, unit_sums, own_grad)
    returned = lax.all_to_all(returning, ("z", "x", "c"), 0, 0, tiled=True)

    totals = lax.psum(totals, "dp")
    kept, sent, done = weight_terms(core.reshape(1), gathered, proj_grad, totals)
    projected = project(core.reshape(1), gathered, mine, other, done)
    got = lax.ppermute(sent, "c", [(0, 1), (1, 0)])
    terms = (kept.astype(f32) + got.astype(f32)).astype(bf16)
    terms, returned = lax.optimization_barrier((terms, returned))
    hidden_grad = hidden_gradient(slot_tile, peers, peers.T, gain, hidden, stats, returned)
    parts = lax.all_to_all(terms, ("z", "x"), split_axis=0, concat_axis=0, tiled=True)
    weight_grad, gain_grad, bias_grad = weight_sum(parts)
    return projected, weight_grad, hidden_grad, gain_grad, bias_grad


def solution(mesh):
    sizes = (mesh.shape["dp"], NZ, NX, NC)
    split = Mesh(mesh.devices.reshape(sizes), ("dp", "z", "x", "c"))
    tile = ("z", "x", "c")
    every = ("dp",) + tile
    return jax.shard_map(
        shards,
        mesh=split,
        in_specs=(
            P(every, None, None),
            P(),
            P(),
            P(every),
            P("dp", None, None, None),
            P(tile, "dp"),
            P(tile, None, "dp"),
        ),
        out_specs=(P(tile, None, "dp"), P(tile, "dp"), P(every, None, None), P(), P()),
        check_vma=False,
    )
```
